32 devices in a mesh: groups: 2 (over x), ctx: 16 (over z, y, core).
Axes of the slice: x: 2, y: 2, z: 4, core: 2. Of those that a mesh axis runs over, the one named last changes fastest.
Arguments:
- query: bfloat16 [8192, 6144], P(('groups', 'ctx')), parts along dimension 0, may hold values from -6 to 6
- key_rows: bfloat16 [8192, 6144], P(('groups', 'ctx')), parts along dimension 0, may hold values from -0.59765625 to 0.59765625
- value_rows: bfloat16 [8192, 6144], P(('groups', 'ctx')), parts along dimension 0, may hold values from -60 to 60
- log_decay: float32 [8192, 48], P(('groups', 'ctx')), parts along dimension 0, may hold values from -1.2 to 0
- gate_input: bfloat16 [8192, 6144], P(('groups', 'ctx')), parts along dimension 0, may hold values from -6 to 6
- residual: bfloat16 [8192, 6144], P(('groups', 'ctx')), parts along dimension 0, may hold values from -60 to 60
- attn_gain: float32 [6144], replicated, may hold values from 0.1 to 1.9
- moe_gain: float32 [6144], replicated, may hold values from 0.1 to 1.9
- expert_ids: int32 [8192, 2], P(('groups', 'ctx')), parts along dimension 0, may hold values from 0 to 15, all different within a row; in each aligned block of 256 rows (0 to 255, 256 to 511, ...) at most 40 rows name the same one
Outputs:
- expert_rows: bfloat16 [32, 640, 6144], P(('groups', 'ctx')), parts along dimension 0
The draws below stay inside these ranges and needn't reach their ends.
There are 2 independent parts, one for each index of `groups`. The reference program is written for one: setup_inputs(seed, part) draws one part's arguments, and reference() takes and returns one part's arrays. A program takes and returns all parts, laid end to end along the dimension named above; an argument that names none is the same for every part. Nothing has to cross between parts.
Inputs may be any that keep to these rules, and one draw needn't show every extreme that they name: `expert_ids`: in the rows of one device (aligned blocks of 256 rows) no expert is named more than 40 times, a bound that some block reaches; the two experts of a row differ.
All inputs are finite; a program needn't handle non-finite values.
Results may differ from the reference program's by a relative error of at most 0.0027.
Values may be sent and summed in bfloat16 or wider, within the bound.
No kernel may reach another device: no remote copies, remote signals or barrier semaphores. Data moves between devices by JAX's collectives and lax.ppermute only.
A program may use at most 256 MiB of HBM per device.

```python
import math
import jax
import jax.numpy as jnp
import numpy as np
from jax import lax

D = 6144
HEAD_DIM = 128
HEAD_GROUP = 48
TOPK = 2
TOK_DEV = 256
PROMPT_TOKENS = 4096
EXPERTS = 16
CAP = 40
N_CTX = 16


def scaled_field(key):
    partition_count = jax.random.split(key, 3)
    column_scale = jnp.exp(jax.random.uniform(partition_count[0], (1, D), jnp.float32, jnp.log(0.3), jnp.log(3.0)))
    row_scale = jnp.exp(jax.random.uniform(partition_count[1], (PROMPT_TOKENS, 1), jnp.float32, jnp.log(0.3), jnp.log(3.0)))
    base = jnp.clip(jax.random.normal(partition_count[2], (PROMPT_TOKENS, D), jnp.float32), -6.0, 6.0)
    return (base * column_scale * row_scale).astype(jnp.bfloat16)


def draw_value_rows(key, part):
    return scaled_field(jax.random.fold_in(key, 11))


def draw_residual(key, part):
    return scaled_field(jax.random.fold_in(key, 23))


def draw_log_decay(key, part):
    partition_count = jax.random.split(jax.random.fold_in(key, 5), 7)
    share = 0.5
    fast_head = jax.random.uniform(partition_count[0], (HEAD_GROUP,), jnp.float32) < share
    slow_rate = jnp.exp(jax.random.uniform(partition_count[1], (HEAD_GROUP,), jnp.float32, jnp.log(0.05), jnp.log(0.25))) / PROMPT_TOKENS
    fast_rate = jnp.exp(jax.random.uniform(partition_count[2], (HEAD_GROUP,), jnp.float32, jnp.log(1.0 / 50.0), jnp.log(1.0 / 30.0)))
    head_decay_rate = jnp.where(fast_head, fast_rate, slow_rate)
    machine_multiplier = jnp.exp(jax.random.uniform(partition_count[3], (PROMPT_TOKENS // TOK_DEV, HEAD_GROUP), jnp.float32, jnp.log(0.5), jnp.log(2.0)))
    machine_multiplier = jnp.repeat(machine_multiplier, TOK_DEV, axis=0)
    random_noise = jax.random.uniform(partition_count[4], (PROMPT_TOKENS, HEAD_GROUP), jnp.float32, 0.5, 1.5)
    spike_positions = jax.random.randint(partition_count[5], (2,), 0, PROMPT_TOKENS)
    spike_penalty = jnp.log(jax.random.uniform(partition_count[6], (2, HEAD_GROUP), jnp.float32, 0.5, 0.8))
    spike_flags = (jnp.arange(PROMPT_TOKENS)[:, None] == spike_positions[None, :]).astype(jnp.float32)
    return -head_decay_rate[None, :] * machine_multiplier * random_noise + spike_flags @ spike_penalty


def block_levels(stream_key, shape, pieces, smallest, top_value):
    loudness = 1.0
    for dim, shards_of in pieces:
        draws = jax.random.uniform(jax.random.fold_in(jax.random.fold_in(stream_key, 6), dim), (shards_of,), jnp.float32, smallest / len(pieces), top_value / len(pieces))
        loudness = loudness * jnp.repeat(jnp.exp(draws), shape[dim] // shards_of).reshape((-1,) + (1,) * (len(shape) - 1 - dim))
    return loudness


def assign_block(own_key, own, number, rows, number_of, top, reach, skew):
    order = jax.random.permutation(own_key, number_of)
    crowded, ordinary = portions_of(number_of, rows * top, reach, skew, True), portions_of(number_of, rows * top, reach, skew, False)
    places = jnp.arange(number_of)

    def named(tallies, offset_by):
        used = int((tallies > 0).sum())
        fixed = max(1, used // 4)
        passed = fixed + (places - fixed + offset_by * (used - fixed)) % max(1, number_of - fixed)
        return jnp.zeros((number_of,), jnp.int32).at[order[jnp.where(places < fixed, places, passed)]].set(jnp.asarray(tallies, jnp.int32))

    tallies = jnp.where(number % 4 == 0, named(crowded, number // 4), named(ordinary, number - number // 4 - 1))
    mixed = jax.random.permutation(jax.random.fold_in(own, 3), number_of)
    source_of, taker = mixed[0:number_of // 2 * 2:2], mixed[1:number_of // 2 * 2:2]
    margin = jnp.minimum(tallies[source_of] - 1, reach - tallies[taker]) // 2
    margin = jnp.where((source_of == order[0]) | (taker == order[0]) | (tallies[taker] == 0), 0, jnp.maximum(margin, 0))
    passed = jax.random.randint(jax.random.fold_in(own, 4), (number_of // 2,), 0, 1 << 20) % (margin + 1)
    tallies = tallies.at[source_of].add(-passed).at[taker].add(passed)
    items = jnp.searchsorted(jnp.cumsum(tallies), jnp.arange(rows * top), side="right").astype(jnp.int32)
    table = items.reshape(top, rows).T
    table = table[jax.random.permutation(jax.random.fold_in(own, 1), rows)]
    offset_by = jax.random.randint(jax.random.fold_in(own, 2), (rows, 1), 0, top)
    return jnp.take_along_axis(table, (jnp.arange(top)[None, :] + offset_by) % top, axis=1)


def portions_of(number_of, total, bound, slope, full):
    loads = [(1 << 20) // math.isqrt(rank ** slope) + 1 for rank in range(1, number_of + 1)]
    largest = bound if full else min(bound, max(-(-total // number_of), total * loads[0] // sum(loads)))
    least = 1 if total - largest >= number_of - 1 else 0
    holding, rest = [largest] + [least] * (number_of - 1), total - largest - least * (number_of - 1)
    while rest > 0:
        free = [i for i in range(1, number_of) if holding[i] < largest] or [i for i in range(1, number_of) if holding[i] < bound]
        mass, left = sum([loads[i] for i in free]), rest
        for i in free:
            more = min(bound - holding[i], max(1, left * loads[i] // mass), rest)
            holding[i] = holding[i] + more
            rest = rest - more
    return np.array(holding)


def centred(rng, shape, scale, reach, pieces=(), kind=jnp.bfloat16):
    values = jax.random.normal(rng, shape, jnp.float32) * scale
    if len(pieces) > 0:
        values = block_levels(rng, shape, pieces, -0.22, 0.18) * values
    return jnp.clip(values, min=-reach, max=reach).astype(kind)


def setup_inputs(seed: int = 0, part: int = 0) -> dict:
    streams_of = jax.random.split(jax.random.key(seed), 10)
    part_keys = jax.random.split(jax.random.fold_in(streams_of[9], part), 10)
    query = centred(part_keys[0], (PROMPT_TOKENS, D), 1.0, 6.0, ((0, 16),))
    key_rows = centred(part_keys[1], (PROMPT_TOKENS, D), 0.1, 0.59765625, ((0, 16),))
    value_rows = draw_value_rows(jax.random.fold_in(jax.random.fold_in(streams_of[9], part), 71), part)
    log_decay = draw_log_decay(jax.random.fold_in(jax.random.fold_in(streams_of[9], part), 71), part)
    gate_input = centred(part_keys[4], (PROMPT_TOKENS, D), 1.0, 6.0, ((0, 16),))
    residual = draw_residual(jax.random.fold_in(jax.random.fold_in(streams_of[9], part), 71), part)
    attn_gain = jnp.clip(1.0 + 0.18 * jax.random.normal(streams_of[6], (D,), jnp.float32), 0.1, 1.9)
    moe_gain = jnp.clip(1.0 + 0.18 * jax.random.normal(streams_of[7], (D,), jnp.float32), 0.1, 1.9)
    expert_ids_keys = jax.random.split(jax.random.fold_in(part_keys[8], 1), PROMPT_TOKENS // TOK_DEV)
    expert_ids_turns = jax.random.permutation(jax.random.fold_in(part_keys[8], 3), PROMPT_TOKENS // TOK_DEV)
    expert_ids = jax.vmap(lambda own, number: assign_block(jax.random.fold_in(part_keys[8], 2), own, number, TOK_DEV, EXPERTS, TOPK, CAP, 2))(expert_ids_keys, expert_ids_turns).reshape((PROMPT_TOKENS, TOPK))
    return {"query": query, "key_rows": key_rows, "value_rows": value_rows, "log_decay": log_decay, "gate_input": gate_input, "residual": residual, "attn_gain": attn_gain, "moe_gain": moe_gain, "expert_ids": expert_ids}


def reference(query, key_rows, value_rows, log_decay, gate_input, residual, attn_gain, moe_gain, expert_ids):
    query_heads = query.reshape(N_CTX, TOK_DEV, HEAD_GROUP, HEAD_DIM)
    key_heads = key_rows.reshape(N_CTX, TOK_DEV, HEAD_GROUP, HEAD_DIM)
    value_heads = value_rows.reshape(N_CTX, TOK_DEV, HEAD_GROUP, HEAD_DIM)
    cumulative = jnp.cumsum(log_decay.reshape(N_CTX, TOK_DEV, HEAD_GROUP), axis=1)

    def block_summary(inputs):
        key_block, value_block, cum_block = inputs
        final_log = cum_block[-1]
        weighted_keys = (jnp.exp(final_log - cum_block)[:, :, None] * key_block.astype(jnp.float32)).astype(jnp.bfloat16)
        block_state = jnp.einsum('thd,the->hde', weighted_keys.astype(jnp.float32), value_block.astype(jnp.float32))
        return (block_state, jnp.exp(final_log))
    states, decays = lax.map(block_summary, (key_heads, value_heads, cumulative))

    def carry_step(previous, inputs):
        block_state, block_decay = inputs
        return (block_decay[:, None, None] * previous + block_state, previous)
    _, carried = lax.scan(carry_step, jnp.zeros((HEAD_GROUP, HEAD_DIM, HEAD_DIM), jnp.float32), (states, decays))
    positions = jnp.arange(TOK_DEV, dtype=jnp.int32)
    causal_mask = positions[:, None] >= positions[None, :]

    def block_output(inputs):
        query_block, key_block, value_block, cum_block, previous = inputs
        score_block = jnp.einsum('thd,shd->hts', query_block.astype(jnp.float32), key_block.astype(jnp.float32))
        cum_heads = cum_block.T
        log_gap = cum_heads[:, :, None] - cum_heads[:, None, :]
        log_gap = jnp.where(causal_mask[None], log_gap, 0.0)
        intra_weights = jnp.where(causal_mask[None], score_block * jnp.exp(log_gap), 0.0).astype(jnp.bfloat16)
        intra_out = jnp.einsum('hts,shd->thd', intra_weights.astype(jnp.float32), value_block.astype(jnp.float32))
        inter_out = jnp.exp(cum_block)[:, :, None] * jnp.einsum('thd,hde->the', query_block.astype(jnp.float32), previous, precision=lax.Precision.HIGHEST)
        return (intra_out + inter_out).reshape(TOK_DEV, D)
    attention = lax.map(block_output, (query_heads, key_heads, value_heads, cumulative, carried)).reshape(PROMPT_TOKENS, D)
    branch_out = attention * lax.rsqrt(lax.optimization_barrier(jnp.mean(attention * attention, axis=-1, keepdims=True)) + 1e-06) * attn_gain * jax.nn.sigmoid(gate_input.astype(jnp.float32))
    hidden_rows = residual.astype(jnp.float32) + branch_out
    normed_rows = (hidden_rows * lax.rsqrt(lax.optimization_barrier(jnp.mean(hidden_rows * hidden_rows, axis=-1, keepdims=True)) + 1e-06) * moe_gain).astype(jnp.bfloat16)
    pair_ids = expert_ids.reshape(N_CTX, TOK_DEV * TOPK)
    one_hot = (pair_ids[:, :, None] == jnp.arange(EXPERTS, dtype=jnp.int32)[None, None, :]).astype(jnp.int32)
    earlier_count = jnp.cumsum(one_hot, axis=1) - one_hot
    slot_index = lax.optimization_barrier(jnp.sum(earlier_count * one_hot, axis=2))
    source_block = jnp.arange(N_CTX, dtype=jnp.int32)[:, None]
    target_row = (pair_ids * (N_CTX * CAP) + source_block * CAP + slot_index).astype(jnp.int32)
    pair_rows = jnp.repeat(normed_rows, TOPK, axis=0)
    gathered = jnp.zeros((EXPERTS * N_CTX * CAP, D), jnp.bfloat16).at[target_row.reshape(-1)].set(pair_rows)
    return gathered.reshape(EXPERTS, N_CTX * CAP, D)
```

```python
import functools
import jax
import jax.numpy as jnp
from jax import lax
from jax.experimental import pallas as pl
from jax.experimental.pallas import tpu as pltpu
from jax.sharding import PartitionSpec as P

EXP_DEV = 1
SLOTS = 4
CHUNKS = 3
EXACT = lax.Precision.HIGHEST
F32 = jnp.float32
BF16 = jnp.bfloat16


def dot(a, b, contract, precision=None):
    return lax.dot_general(
        a, b, ((contract[:1], contract[1:]), ((), ())), precision=precision, preferred_element_type=F32
    )


def group_decay(ld_ref, first, count):
    heads = ld_ref.shape[1]
    row = lax.broadcasted_iota(jnp.int32, (heads, count), 0)
    col = lax.broadcasted_iota(jnp.int32, (heads, count), 1)
    pick = (row == first + col).astype(F32)
    return dot(ld_ref[...], pick, (1, 0), EXACT)


def running(ld):
    tok = ld.shape[0]
    row = lax.broadcasted_iota(jnp.int32, (tok, tok), 0)
    col = lax.broadcasted_iota(jnp.int32, (tok, tok), 1)
    return dot((row >= col).astype(F32), ld, (1, 0), EXACT)


def running_rows(ld):
    tok = ld.shape[0]
    row = lax.broadcasted_iota(jnp.int32, (tok, tok), 0)
    col = lax.broadcasted_iota(jnp.int32, (tok, tok), 1)
    return dot(ld, (row <= col).astype(F32), (0, 0), EXACT)


def state_kernel(first_slot, hd, place, k_ref, v_ref, ld_ref, *outs):
    gh = k_ref.shape[1] // hd
    group = jnp.bitwise_xor(pl.program_id(0) + first_slot, place[0])
    cum = running(group_decay(ld_ref, group * gh, gh))
    weight = jnp.exp(cum[-1:, :] - cum)
    per = gh // len(outs)
    for i in range(gh):
        cols = slice(i * hd, (i + 1) * hd)
        wk = (weight[:, i : i + 1] * k_ref[:, cols].astype(F32)).astype(BF16)
        outs[i // per][0, i % per] = dot(wk, v_ref[:, cols], (0, 0))


def block_states(place, key_rows, value_rows, log_decay, first_slot, hd):
    tok, width = key_rows.shape
    gw = width // SLOTS
    gh = gw // hd
    per = gh // CHUNKS
    cols = lambda i, s: (0, jnp.bitwise_xor(i + first_slot, s[0]))
    return pl.pallas_call(
        functools.partial(state_kernel, first_slot, hd),
        grid_spec=pltpu.PrefetchScalarGridSpec(
            num_scalar_prefetch=1,
            grid=(2,),
            in_specs=[
                pl.BlockSpec((tok, gw), cols),
                pl.BlockSpec((tok, gw), cols),
                pl.BlockSpec(log_decay.shape, lambda i, s: (0, 0)),
            ],
            out_specs=[pl.BlockSpec((1, per, hd, hd), lambda i, s: (i, 0, 0, 0))] * CHUNKS,
        ),
        out_shape=[jax.ShapeDtypeStruct((2, per, hd, hd), F32)] * CHUNKS,
        compiler_params=pltpu.CompilerParams(vmem_limit_bytes=32 << 20),
        cost_estimate=pl.CostEstimate(
            flops=tok * width * hd, bytes_accessed=2 * tok * width + 2 * width * hd, transcendentals=tok * width // hd
        ),
        name="block_states",
    )(place, key_rows, value_rows, log_decay)


def intra_kernel(hd, q_ref, k_ref, v_ref, ld_ref, o_ref):
    tok = q_ref.shape[0]
    gh = q_ref.shape[1] // hd
    half = tok // 2
    ld = group_decay(ld_ref, pl.program_id(0) * gh, gh)
    cum = running(ld)
    cum_rows = running_rows(ld)
    for i in range(gh):
        cols = slice(i * hd, (i + 1) * hd)
        for first, seen in ((0, half), (half, tok)):
            score = dot(q_ref[first : first + half, cols], k_ref[:seen, cols], (1, 1))
            gap = cum[first : first + half, i : i + 1] - cum_rows[i : i + 1, :seen]
            row = lax.broadcasted_iota(jnp.int32, (half, seen), 0) + first
            col = lax.broadcasted_iota(jnp.int32, (half, seen), 1)
            weights = jnp.where(row >= col, score * jnp.exp(gap), 0.0).astype(BF16)
            o_ref[first : first + half, cols] = dot(weights, v_ref[:seen, cols], (1, 0))


def intra(query, key_rows, value_rows, log_decay, hd):
    tok, width = query.shape
    steps = 8
    block = pl.BlockSpec((tok, width // steps), lambda i: (0, i))
    return pl.pallas_call(
        functools.partial(intra_kernel, hd),
        grid=(steps,),
        in_specs=[block, block, block, pl.BlockSpec(log_decay.shape, lambda i: (0, 0))],
        out_specs=block,
        out_shape=jax.ShapeDtypeStruct((tok, width), F32),
        compiler_params=pltpu.CompilerParams(vmem_limit_bytes=32 << 20),
        cost_estimate=pl.CostEstimate(
            flops=3 * tok * tok * width, bytes_accessed=10 * tok * width, transcendentals=tok * tok * width // hd
        ),
        name="intra",
    )(query, key_rows, value_rows, log_decay)


def finish_kernel(
    hd, cap, row_steps, out_steps, place, q_ref, in_ref, ld_ref, gate_ref, res_ref, ag_ref, mg_ref, ids_ref, *rest
):
    states = rest[: 2 * CHUNKS]
    o_ref, att, normed, target = rest[2 * CHUNKS :]
    tok, width = att.shape
    gh = q_ref.shape[1] // hd
    per = gh // CHUNKS
    step = pl.program_id(0)

    for slot in range(SLOTS):

        @pl.when(step == slot)
        def _():
            group = jnp.bitwise_xor(slot, place[0])
            grow = jnp.exp(running(group_decay(ld_ref, group * gh, gh)))
            for i in range(gh):
                cols = slice(i * hd, (i + 1) * hd)
                carried = states[(slot // 2) * CHUNKS + i // per][slot % 2, i % per]
                high = carried.astype(BF16)
                low = (carried - high.astype(F32)).astype(BF16)
                q = q_ref[:, cols]
                inter = dot(q, high, (1, 0)) + dot(q, low, (1, 0))
                where = pl.ds(pl.multiple_of(group * (gh * hd) + i * hd, hd), hd)
                att[:, where] = in_ref[:, cols] + grow[:, i : i + 1] * inter

    rows = tok // row_steps

    @pl.when((step >= SLOTS) & (step < SLOTS + row_steps))
    def _():
        at = pl.ds(pl.multiple_of((step - SLOTS) * rows, rows), rows)
        a = att[at, :]
        scale = lax.rsqrt(jnp.mean(a * a, axis=-1, keepdims=True) + 1e-06)
        branch = a * scale * ag_ref[...] * jax.nn.sigmoid(gate_ref[...].astype(F32))
        hidden = res_ref[...].astype(F32) + branch
        scale = lax.rsqrt(jnp.mean(hidden * hidden, axis=-1, keepdims=True) + 1e-06)
        normed[at, :] = (hidden * scale * mg_ref[...]).astype(BF16)

    @pl.when(step == SLOTS + row_steps)
    def _():
        top = ids_ref.shape[0]
        experts = out_steps * o_ref.shape[0] // cap
        ids = ids_ref[...]
        expert = lax.broadcasted_iota(jnp.int32, (experts, tok), 0)
        hot = [(ids[k : k + 1, :] == expert).astype(F32) for k in range(top)]
        row = lax.broadcasted_iota(jnp.int32, (tok, tok), 0)
        col = lax.broadcasted_iota(jnp.int32, (tok, tok), 1)
        count = dot(sum(hot).astype(BF16), (row < col).astype(BF16), (1, 0))
        for k in range(top):
            slot = jnp.sum(hot[k] * count, axis=0, keepdims=True).astype(jnp.int32)
            target[k : k + 1, :] = ids[k : k + 1, :] * cap + slot
            count = count + hot[k]

    @pl.when(step >= SLOTS + row_steps)
    def _():
        out_rows = o_ref.shape[0]
        base = (step - SLOTS - row_steps) * out_rows
        row = lax.broadcasted_iota(jnp.int32, (out_rows, tok), 0) + base
        hit = row == target[0:1, :]
        for k in range(1, ids_ref.shape[0]):
            hit = hit | (row == target[k : k + 1, :])
        pick = hit.astype(F32).astype(BF16)
        part = width // 4
        for n in range(4):
            cols = slice(n * part, (n + 1) * part)
            o_ref[:, cols] = dot(pick, normed[:, cols], (1, 0)).astype(BF16)


def finish(place, query, intra_out, log_decay, gate, residual, attn_gain, moe_gain, ids, states, cap, experts, hd):
    tok, width = query.shape
    gw = width // SLOTS
    row_steps, out_steps = 4, 4
    out_rows = experts * cap // out_steps
    last = SLOTS - 1
    cols = lambda i, s: (0, jnp.bitwise_xor(jnp.minimum(i, last), s[0]))
    rows = lambda i, s: (jnp.clip(i - SLOTS, 0, row_steps - 1), 0)
    whole = lambda i, s: (0, 0)
    return pl.pallas_call(
        functools.partial(finish_kernel, hd, cap, row_steps, out_steps),
        grid_spec=pltpu.PrefetchScalarGridSpec(
            num_scalar_prefetch=1,
            grid=(SLOTS + row_steps + out_steps,),
            in_specs=[
                pl.BlockSpec((tok, gw), cols),
                pl.BlockSpec((tok, gw), cols),
                pl.BlockSpec(log_decay.shape, whole),
                pl.BlockSpec((tok // row_steps, width), rows),
                pl.BlockSpec((tok // row_steps, width), rows),
                pl.BlockSpec((1, width), whole),
                pl.BlockSpec((1, width), whole),
                pl.BlockSpec(ids.shape, whole),
            ]
            + [pl.BlockSpec(s.shape, lambda i, s: (0, 0, 0, 0)) for s in states],
            out_specs=pl.BlockSpec((out_rows, width), lambda i, s: (jnp.maximum(i - SLOTS - row_steps, 0), 0)),
            scratch_shapes=[
                pltpu.VMEM((tok, width), F32),
                pltpu.VMEM((tok, width), BF16),
                pltpu.VMEM((8, tok), jnp.int32),
            ],
        ),
        out_shape=jax.ShapeDtypeStruct((experts * cap, width), BF16),
        compiler_params=pltpu.CompilerParams(vmem_limit_bytes=48 << 20),
        cost_estimate=pl.CostEstimate(
            flops=4 * tok * width * hd, bytes_accessed=20 * tok * width, transcendentals=tok * width
        ),
        name="finish",
    )(place, query, intra_out, log_decay, gate, residual, attn_gain[None], moe_gain[None], ids, *states)


def swap(value, bit):
    size = lax.axis_size("ctx")
    return lax.ppermute(value, "ctx", [(i, i ^ bit) for i in range(size)])


def carried_states(index, place, keep, send, log_decay):
    size = lax.axis_size("ctx")
    rows = size // SLOTS
    core, side = index % 2, (index // 2) % 2
    heads = log_decay.shape[1]
    own = jnp.exp(jnp.sum(log_decay, axis=0))
    decay = jnp.stack([own, swap(own, 1), swap(own, 2), swap(own, 3)]).reshape(4, SLOTS, CHUNKS, -1)
    near = [lax.dynamic_index_in_dim(decay, jnp.bitwise_xor(j, place), 1, keepdims=False) for j in range(2)]
    near = jnp.stack(near, axis=1)[..., None, None]
    one = jnp.float32(1)

    received = [swap(s, 1) for s in send]
    mine, rest = [], []
    for k in range(CHUNKS):
        d_own, d_core = near[0, :, k], near[1, :, k]
        total = jnp.where(core == 0, d_core, one) * keep[k] + jnp.where(core == 0, one, d_own) * received[k]
        first = jnp.where(core == 0, keep[k], received[k])
        d_first = jnp.where(core == 0, d_own, d_core)
        chip = d_own[0] * d_core[0]
        chip_other = near[2, 0, k] * near[3, 0, k]
        other = swap(total[1], 2)
        row_total = jnp.where(side == 0, chip_other, one) * total[0] + jnp.where(side == 0, one, chip) * other
        row_decay = chip * chip_other
        upper = jnp.where(side == 0, total[0], other)
        d_upper = jnp.where(side == 0, chip, chip_other)
        before = jnp.zeros_like(row_total)
        for s in range(rows - 1):
            pairs = [(s * SLOTS + j, (s + 1) * SLOTS + j) for j in range(SLOTS)]
            before = before + lax.ppermute(row_decay * before + row_total, "ctx", pairs)
        lower = d_upper * before + upper
        there = swap(jnp.where(side == 0, lower, before), 2)
        here = jnp.where(side == 0, before, lower)
        pair = jnp.stack([here, there])
        second = d_first * pair + first
        rest.append(swap(jnp.where(core == 0, second, pair), 1))
        mine.append(jnp.where(core == 0, pair, second))
    return mine + rest


def body(
    query, key_rows, value_rows, log_decay, gate_input, residual, attn_gain, moe_gain, expert_ids
):
    tok_rows, model_width = query.shape
    hd = model_width // log_decay.shape[1]
    index = lax.axis_index("ctx")
    place = (index % 2) * 2 + (index // 2) % 2
    place_ref = place.astype(jnp.int32)[None]
    send = block_states(place_ref, key_rows, value_rows, log_decay, 2, hd)
    keep = block_states(place_ref, key_rows, value_rows, log_decay, 0, hd)
    states = carried_states(index, place, keep, send, log_decay)
    intra_out = intra(query, key_rows, value_rows, log_decay, hd)
    top_count = expert_ids.shape[1]
    expert_count = EXP_DEV * lax.axis_size("ctx")
    capacity = 5 * tok_rows * top_count // (4 * expert_count)
    outgoing = finish(
        place_ref, query, intra_out, log_decay, gate_input, residual, attn_gain, moe_gain,
        expert_ids.T, states, capacity, expert_count, hd,
    )
    arrived = lax.all_to_all(outgoing, "ctx", split_axis=0, concat_axis=0, tiled=True)
    return arrived[None]


def solution(mesh):
    rows = P(("groups", "ctx"), None)
    in_specs = (rows, rows, rows, rows, rows, rows, P(), P(), rows)
    out_specs = P(("groups", "ctx"), None, None)
    return jax.shard_map(body, mesh=mesh, in_specs=in_specs, out_specs=out_specs, check_vma=False)
```

```python
import functools
import jax
import jax.numpy as jnp
from jax import lax
from jax.experimental import pallas as pl
from jax.experimental.pallas import tpu as pltpu
from jax.sharding import PartitionSpec as P

EXP_DEV = 1
SLOTS = 4
CHUNKS = 2
WIRE = jnp.float32
LANES = 128
TAIL = 8
F32 = jnp.float32
BF16 = jnp.bfloat16
ANY = pl.BlockSpec(memory_space=pl.ANY)
VMEM = pl.BlockSpec(memory_space=pltpu.VMEM)
SMEM = pl.BlockSpec(memory_space=pltpu.SMEM)
BRIEF = pl.CostEstimate(flops=1, bytes_accessed=1, transcendentals=0)


def dot(a, b, contract=(1, 0)):
    return lax.dot_general(a, b, ((contract[:1], contract[1:]), ((), ())), preferred_element_type=F32)


def running(ld_ref, group, count):
    ld = ld_ref[:count, :]
    for g in range(1, ld_ref.shape[0] // count):
        ld = jnp.where(group == g, ld_ref[g * count : (g + 1) * count, :], ld)
    tok = ld.shape[1]
    row = lax.broadcasted_iota(jnp.int32, (tok, tok), 0)
    col = lax.broadcasted_iota(jnp.int32, (tok, tok), 1)
    upper = (row <= col).astype(F32).astype(BF16)
    high = ld.astype(BF16)
    rest = ld - high.astype(F32)
    mid = rest.astype(BF16)
    low = (rest - mid.astype(F32)).astype(BF16)
    return dot(high, upper) + (dot(mid, upper) + dot(low, upper))


def state_kernel(first_slot, hd, place, k_hbm, v_hbm, ld_ref, dep, *rest):
    outs = rest[:CHUNKS]
    k_ref, v_ref, sems = rest[CHUNKS:]
    gw = k_ref.shape[2]
    gh = gw // hd
    per = gh // CHUNKS
    copies = []
    for j in range(2):
        at = pl.ds(pl.multiple_of(jnp.bitwise_xor(j + first_slot, place[0]) * gw, gw), gw)
        copies.append(
            [
                pltpu.make_async_copy(k_hbm.at[:, at], k_ref.at[j], sems.at[2 * j]),
                pltpu.make_async_copy(v_hbm.at[:, at], v_ref.at[j], sems.at[2 * j + 1]),
            ]
        )
        for c in copies[j]:
            c.start()
    for j in range(2):
        cum = running(ld_ref, jnp.bitwise_xor(j + first_slot, place[0]), gh)
        total = cum[:, -1:]
        weight = jnp.exp(total - cum)
        decay = jnp.exp(total)
        for c in copies[j]:
            c.wait()
        for i in range(gh):
            cols = slice(i * hd, (i + 1) * hd)
            wk = (weight[i : i + 1, :] * k_ref[j, :, cols].T.astype(F32)).astype(BF16)
            out = outs[i // per]
            out[j, i % per, :hd, :] = dot(wk, v_ref[j, :, cols])
            out[j, i % per, hd:, :] = jnp.broadcast_to(decay[i : i + 1, :], (TAIL, hd))


def block_states(place, key_rows, value_rows, log_decay, dep, first_slot, hd):
    tok, width = key_rows.shape
    gw = width // SLOTS
    per = gw // hd // CHUNKS
    shape = (2, per, hd + TAIL, hd)
    hbm = pl.BlockSpec(memory_space=pltpu.HBM)
    vmem = pl.BlockSpec(memory_space=pltpu.VMEM)
    return pl.pallas_call(
        functools.partial(state_kernel, first_slot, hd),
        in_specs=[pl.BlockSpec(memory_space=pltpu.SMEM), hbm, hbm, vmem, ANY],
        out_specs=[vmem] * CHUNKS,
        scratch_shapes=[
            pltpu.VMEM((2, tok, gw), BF16),
            pltpu.VMEM((2, tok, gw), BF16),
            pltpu.SemaphoreType.DMA((4,)),
        ],
        out_shape=[jax.ShapeDtypeStruct(shape, F32)] * CHUNKS,
        compiler_params=pltpu.CompilerParams(vmem_limit_bytes=60 << 20),
        cost_estimate=BRIEF,
        name="block_states",
    )(place, key_rows, value_rows, log_decay, dep)


def intra_kernel(hd, slot, place, q_ref, k_ref, v_ref, ld_ref, dep, *outs):
    tok = q_ref.shape[0]
    gh = q_ref.shape[1] // hd
    half = tok // 2
    cum_rows = running(ld_ref, jnp.bitwise_xor(slot, place[0]), gh)
    cum = cum_rows.T
    row = lax.broadcasted_iota(jnp.int32, (half, half), 0)
    col = lax.broadcasted_iota(jnp.int32, (half, half), 1)
    causal = row >= col
    per = gh // len(outs)
    for i in range(gh):
        cols = slice(i * hd, (i + 1) * hd)
        o_ref, to = outs[i // per], slice(i % per * hd, (i % per + 1) * hd)
        down, across = cum[:, i : i + 1], cum_rows[i : i + 1, :]
        parts = []
        for first in (0, half):
            at = slice(first, first + half)
            score = dot(q_ref[at, cols], k_ref[at, cols], (1, 1))
            weights = jnp.where(causal, score * jnp.exp(down[at] - across[:, at]), 0.0).astype(BF16)
            parts.append(dot(weights, v_ref[at, cols]))
        o_ref[:half, to] = parts[0]
        middle = across[:, half - 1 : half]
        score = dot(q_ref[half:, cols], k_ref[:half, cols], (1, 1))
        weights = (score * (jnp.exp(down[half:] - middle) * jnp.exp(middle - across[:, :half]))).astype(BF16)
        o_ref[half:, to] = parts[1] + dot(weights, v_ref[:half, cols])


def intra(place, query, key_rows, value_rows, log_decay, dep, slot, hd):
    tok, width = query.shape
    gw = width // SLOTS
    block = pl.BlockSpec((tok, gw), lambda i, s: (0, jnp.bitwise_xor(slot, s[0])))
    return pl.pallas_call(
        functools.partial(intra_kernel, hd, slot),
        grid_spec=pltpu.PrefetchScalarGridSpec(
            num_scalar_prefetch=1,
            grid=(1,),
            in_specs=[block, block, block, pl.BlockSpec(log_decay.shape, lambda i, s: (0, 0)), ANY],
            out_specs=[pl.BlockSpec((tok, gw // CHUNKS), lambda i, s: (0, 0))] * CHUNKS,
        ),
        out_shape=[jax.ShapeDtypeStruct((tok, gw // CHUNKS), F32)] * CHUNKS,
        compiler_params=pltpu.CompilerParams(vmem_limit_bytes=16 << 20),
        cost_estimate=BRIEF,
        name="intra",
    )(place, query, key_rows, value_rows, log_decay, dep)


def add_branch(hd, place, slot, first, q_ref, in_ref, ld_ref, gate, gain, states, put):
    own, there = states
    per = own.shape[1]
    grow = jnp.exp(running(ld_ref, jnp.bitwise_xor(slot, place[0]), per * CHUNKS)[first : first + per]).T
    squares = 0.0
    for i in range(per):
        cols = slice(i * hd, (i + 1) * hd)
        carried = (own if slot < 2 else there)[slot % 2, i]
        high = carried.astype(BF16)
        low = (carried - high.astype(F32)).astype(BF16)
        q = q_ref[:, cols]
        att = in_ref[:, cols] + grow[:, i : i + 1] * (dot(q, high) + dot(q, low))
        squares = squares + att * att
        put(cols, att * gain[:, cols] * jax.nn.sigmoid(gate[:, cols].astype(F32)))
    return squares


def branch_kernel(hd, chunk, per, place, q_ref, gate_ref, ag_ref, ld_ref, own, there, dep, *rest):
    ins = rest[:SLOTS]
    o_ref, sq_ref = rest[SLOTS:]
    step = pl.program_id(0)
    for slot in range(SLOTS):

        @pl.when(step == slot)
        def _():
            def put(cols, value):
                o_ref[:, cols] = value

            squares = add_branch(
                hd, place, slot, chunk * per, q_ref, ins[slot], ld_ref, gate_ref, ag_ref, (own, there), put
            )
            sq_ref[...] = squares if slot == 0 else sq_ref[...] + squares


def chunk_block(rows, per, hd, chunk, last):
    return pl.BlockSpec(
        (rows, per * hd),
        lambda i, s: (0, jnp.bitwise_xor(jnp.minimum(i, last), s[0]) * CHUNKS + chunk),
    )


def branch(place, query, gate, attn_gain, log_decay, states, intra_outs, dep, chunk, hd):
    tok, width = query.shape
    per = states[0].shape[1]
    col = lambda rows: chunk_block(rows, per, hd, chunk, SLOTS - 1)
    whole = lambda a: pl.BlockSpec(a.shape, lambda i, s: (0,) * a.ndim)
    part = pl.BlockSpec((tok, per * hd), lambda i, s: (0, 0))
    return pl.pallas_call(
        functools.partial(branch_kernel, hd, chunk, per),
        grid_spec=pltpu.PrefetchScalarGridSpec(
            num_scalar_prefetch=1,
            grid=(SLOTS,),
            in_specs=[col(tok), col(tok), col(1), whole(log_decay), whole(states[0]), whole(states[1]), ANY]
            + [part] * SLOTS,
            out_specs=[
                pl.BlockSpec((tok, per * hd), lambda i, s: (0, i)),
                pl.BlockSpec((tok, hd), lambda i, s: (0, 0)),
            ],
        ),
        out_shape=[
            jax.ShapeDtypeStruct((tok, SLOTS * per * hd), F32),
            jax.ShapeDtypeStruct((tok, hd), F32),
        ],
        compiler_params=pltpu.CompilerParams(vmem_limit_bytes=24 << 20),
        cost_estimate=BRIEF,
        name="branch",
    )(place, query, gate, attn_gain, log_decay, *states, dep, *intra_outs)


def finish_kernel(hd, cap, per, row_steps, place, q_ref, gate_ref, ag_ref, ld_ref, own, there, dep, *rest):
    ins, rest = rest[:SLOTS], rest[SLOTS:]
    early, rest = rest[: CHUNKS - 1], rest[CHUNKS - 1 :]
    squares, rest = rest[: CHUNKS - 1], rest[CHUNKS - 1 :]
    res_ref, mg_ref, ids_ref, o_ref, late, sq, hidden, normed, target = rest
    tok, width = normed.shape
    step = pl.program_id(0)
    cw = per * hd

    for slot in range(SLOTS):

        @pl.when(step == slot)
        def _():
            def put(cols, value):
                late[:, slot * cw + cols.start : slot * cw + cols.stop] = value

            part = add_branch(
                hd, place, slot, (CHUNKS - 1) * per, q_ref, ins[slot], ld_ref, gate_ref, ag_ref, (own, there), put
            )
            if slot == 0:
                for s in squares:
                    part = part + s[...]
                sq[...] = part
            else:
                sq[...] += part

    rows = tok // row_steps

    @pl.when((step >= SLOTS) & (step < SLOTS + row_steps))
    def _():
        at = pl.ds(pl.multiple_of((step - SLOTS) * rows, rows), rows)
        scale = lax.rsqrt(jnp.sum(sq[at, :], axis=-1, keepdims=True) / width + 1e-06)
        total = jnp.zeros((rows, LANES), F32)
        for slot in range(SLOTS):
            group = jnp.bitwise_xor(slot, place[0])
            for k in range(CHUNKS):
                for n in range(cw // LANES):
                    here = slice(slot * cw + n * LANES, slot * cw + (n + 1) * LANES)
                    where = pl.ds(pl.multiple_of((group * CHUNKS + k) * cw + n * LANES, LANES), LANES)
                    value = early[k][:, here] if k < CHUNKS - 1 else late[at, here]
                    value = res_ref[:, where].astype(F32) + value * scale
                    total = total + value * value
                    hidden[:, where] = value
        scale = lax.rsqrt(jnp.sum(total, axis=-1, keepdims=True) / width + 1e-06)
        for n in range(width // LANES):
            cols = slice(n * LANES, (n + 1) * LANES)
            normed[at, cols] = (hidden[:, cols] * scale * mg_ref[:, cols]).astype(BF16)

    @pl.when(step == 0)
    def _():
        top = ids_ref.shape[0]
        experts = target.shape[0] - 8
        ids = ids_ref[...]
        expert = lax.broadcasted_iota(jnp.int32, (experts, tok), 0)
        hot = [(ids[k : k + 1, :] == expert).astype(F32) for k in range(top)]
        row = lax.broadcasted_iota(jnp.int32, (tok, tok), 0)
        col = lax.broadcasted_iota(jnp.int32, (tok, tok), 1)
        count = dot(sum(hot).astype(BF16), (row < col).astype(F32).astype(BF16))
        for k in range(top):
            slot = jnp.sum(hot[k] * count, axis=0, keepdims=True).astype(jnp.int32)
            target[k : k + 1, :] = ids[k : k + 1, :] * cap + slot
            count = count + hot[k]

    @pl.when(step >= SLOTS + row_steps)
    def _():
        out_rows = o_ref.shape[0]
        base = (step - SLOTS - row_steps) * out_rows
        row = lax.broadcasted_iota(jnp.int32, (out_rows, tok), 0) + base
        hit = row == target[0:1, :]
        for k in range(1, ids_ref.shape[0]):
            hit = hit | (row == target[k : k + 1, :])
        pick = hit.astype(F32).astype(BF16)
        part = width // 4
        for n in range(4):
            cols = slice(n * part, (n + 1) * part)
            o_ref[:, cols] = dot(pick, normed[:, cols]).astype(BF16)


def finish(
    place, query, gate, attn_gain, log_decay, states, intra_outs, early, squares, residual, moe_gain, ids, dep, cap, experts, hd
):
    tok, width = query.shape
    per = states[0].shape[1]
    cw = per * hd
    row_steps, out_steps = 4, 4
    out_rows = experts * cap // out_steps
    rows = tok // row_steps
    chunk = CHUNKS - 1
    col = lambda r: chunk_block(r, per, hd, chunk, SLOTS - 1)
    whole = lambda a: pl.BlockSpec(a.shape, lambda i, s: (0,) * a.ndim)
    part = pl.BlockSpec((tok, cw), lambda i, s: (0, 0))
    by_row = lambda w: pl.BlockSpec((rows, w), lambda i, s: (jnp.clip(i - SLOTS, 0, row_steps - 1), 0))
    return pl.pallas_call(
        functools.partial(finish_kernel, hd, cap, per, row_steps),
        grid_spec=pltpu.PrefetchScalarGridSpec(
            num_scalar_prefetch=1,
            grid=(SLOTS + row_steps + out_steps,),
            in_specs=[col(tok), col(tok), col(1), whole(log_decay), whole(states[0]), whole(states[1]), ANY]
            + [part] * SLOTS
            + [by_row(SLOTS * cw)] * len(early)
            + [whole(squares[0])] * len(squares)
            + [by_row(width), whole(moe_gain), whole(ids)],
            out_specs=pl.BlockSpec((out_rows, width), lambda i, s: (jnp.maximum(i - SLOTS - row_steps, 0), 0)),
            scratch_shapes=[
                pltpu.VMEM((tok, SLOTS * cw), F32),
                pltpu.VMEM((tok, hd), F32),
                pltpu.VMEM((rows, width), F32),
                pltpu.VMEM((tok, width), BF16),
                pltpu.VMEM((experts + 8, tok), jnp.int32),
            ],
        ),
        out_shape=jax.ShapeDtypeStruct((experts * cap, width), BF16),
        compiler_params=pltpu.CompilerParams(vmem_limit_bytes=32 << 20),
        cost_estimate=BRIEF,
        name="finish",
    )(place, query, gate, attn_gain, log_decay, *states, dep, *intra_outs, *early, *squares, residual, moe_gain, ids)


def land_kernel(i_ref, o_ref):
    o_ref[0] = i_ref[...]


def land(arrived):
    rows, width = arrived.shape
    steps = 8
    return pl.pallas_call(
        land_kernel,
        grid=(steps,),
        in_specs=[pl.BlockSpec((rows // steps, width), lambda i: (i, 0))],
        out_specs=pl.BlockSpec((1, rows // steps, width), lambda i: (0, i, 0)),
        out_shape=jax.ShapeDtypeStruct((1, rows, width), arrived.dtype),
        cost_estimate=BRIEF,
        compiler_params=pltpu.CompilerParams(vmem_limit_bytes=16 << 20),
        name="land",
    )(arrived)


def swap(value, bit):
    size = lax.axis_size("ctx")
    return lax.ppermute(value, "ctx", [(i, i ^ bit) for i in range(size)])


def small(kernel, name, flags, ins, dep, outs):
    return pl.pallas_call(
        kernel,
        in_specs=[SMEM] + [VMEM] * len(ins) + [ANY],
        out_specs=[VMEM] * len(outs),
        out_shape=[jax.ShapeDtypeStruct(shape, kind) for shape, kind in outs],
        compiler_params=pltpu.CompilerParams(vmem_limit_bytes=16 << 20),
        cost_estimate=BRIEF,
        name=name,
    )(flags, *ins, dep)


def later(before, decay, state):
    return decay * before + state


def decay_rows(decay, rows):
    high = decay.astype(BF16).astype(F32)
    mid = (decay - high).astype(BF16).astype(F32)
    low = decay - high - mid
    row = lax.broadcasted_iota(jnp.int32, (decay.shape[0], rows, decay.shape[2]), 1)
    return jnp.where(row == 0, high, jnp.where(row == 1, mid, jnp.where(row == 2, low, 0.0)))


def chip_kernel(flags, keep, received, dep, mine, sent):
    hd = keep.shape[-1]
    low = flags[1] == 0
    for slot in range(2):
        a = jnp.where(low, keep[slot], received[slot])
        b = jnp.where(low, received[slot], keep[slot])
        state = later(a[:, :hd, :], b[:, hd : hd + 1, :], b[:, :hd, :])
        decay = a[:, hd:, :] * b[:, hd:, :]
        if slot == 0:
            mine[:, :hd, :] = state
            mine[:, hd:, :] = decay
        else:
            sent[:, :hd, :] = state.astype(WIRE)
            sent[:, hd:, :] = decay_rows(decay[:, :1, :], 2 * TAIL).astype(WIRE)


def row_parts(flags, mine, other):
    hd = mine.shape[-1]
    low = flags[2] == 0
    a = (mine[:, :hd, :], mine[:, hd : hd + 1, :])
    b = (other[:, :hd, :].astype(F32), jnp.sum(other[:, hd:, :].astype(F32), axis=1, keepdims=True))
    first = tuple(jnp.where(low, x, y) for x, y in zip(a, b))
    second = tuple(jnp.where(low, y, x) for x, y in zip(a, b))
    return first, second


def row_kernel(flags, mine, other, dep, total, sent):
    hd = mine.shape[-1]
    first, second = row_parts(flags, mine, other)
    state = later(first[0], second[1], second[0])
    total[:, :hd, :] = state
    total[:, hd:, :] = jnp.broadcast_to(first[1] * second[1], (total.shape[0], TAIL, hd))
    sent[...] = state.astype(sent.dtype)


def arrived_sum(refs):
    return sum(r[...].astype(F32) for r in refs)


def hop_kernel(flags, total, *rest):
    hops, sent = rest[:-2], rest[-1]
    hd = total.shape[-1]
    sent[...] = later(arrived_sum(hops), total[:, hd : hd + 1, :], total[:, :hd, :]).astype(sent.dtype)


def side_kernel(flags, mine, other, *rest):
    hops, (_, here, sent) = rest[:-3], rest[-3:]
    low = flags[2] == 0
    first, _ = row_parts(flags, mine, other)
    before = arrived_sum(hops)
    entered = later(before, first[1], first[0])
    here[...] = jnp.where(low, before, entered)
    sent[...] = jnp.where(low, entered, before).astype(sent.dtype)


def core_kernel(flags, keep, received, here, there, dep, own, sent):
    hd = keep.shape[-1]
    low = flags[1] == 0
    for slot, ref in ((0, here), (1, there)):
        pair = ref[...].astype(F32)
        first = jnp.where(low, keep[slot], received[slot])
        second = later(pair, first[:, hd : hd + 1, :], first[:, :hd, :])
        own[slot] = jnp.where(low, pair, second)
        sent[slot] = jnp.where(low, second, pair)


def body(
    query, key_rows, value_rows, log_decay, gate_input, residual, attn_gain, moe_gain, expert_ids
):
    tok_rows, model_width = query.shape
    heads = log_decay.shape[1]
    hd = model_width // heads
    per = heads // SLOTS // CHUNKS
    size = lax.axis_size("ctx")
    hops = size // SLOTS - 1
    index = lax.axis_index("ctx").astype(jnp.int32)
    core, side = jnp.bitwise_and(index, 1), jnp.bitwise_and(lax.shift_right_logical(index, 1), 1)
    place = (2 * core + side)[None]
    flags = jnp.stack([2 * core + side, core, side])
    ld = log_decay.T
    ag, mg = attn_gain[None], moe_gain[None]
    full, wire, plain = (per, hd + TAIL, hd), (per, hd + 2 * TAIL, hd), (per, hd, hd)

    send = block_states(place, key_rows, value_rows, ld, ld, 2, hd)
    received = [swap(s, 1) for s in send]
    keep = block_states(place, key_rows, value_rows, ld, send[0], 0, hd)
    dep = keep[0]
    mine, other = [], []
    for k in range(CHUNKS):
        m, t = small(chip_kernel, "chip", flags, [keep[k], received[k]], dep, [(full, F32), (wire, WIRE)])
        dep = m
        mine.append(m)
        other.append(swap(t, 2))

    intra_outs = []
    totals, arrived = [None] * CHUNKS, [[] for _ in range(CHUNKS)]
    here, there, states = [None] * CHUNKS, [None] * CHUNKS, [None] * CHUNKS
    early, squares = [], []

    def more_intra(dep):
        if len(intra_outs) < SLOTS:
            intra_outs.append(intra(place, query, key_rows, value_rows, ld, dep, len(intra_outs), hd))
            dep = intra_outs[-1][0]
        return dep

    def hop(k, sent):
        s = len(arrived[k])
        pairs = [(s * SLOTS + j, (s + 1) * SLOTS + j) for j in range(SLOTS)]
        arrived[k].append(lax.ppermute(sent, "ctx", pairs))

    dep = more_intra(dep)
    for wave in range(hops + CHUNKS + 2):
        ready = [(k, wave - k) for k in range(CHUNKS) if 0 <= wave - k <= hops + 2]
        for k, stage in sorted(ready, key=lambda r: (r[1] == hops + 2, r[0])):
            if stage == 0:
                totals[k], dep = small(
                    row_kernel, "row", flags, [mine[k], other[k]], dep, [(full, F32), (plain, BF16)]
                )
                hop(k, dep)
            elif stage < hops:
                (dep,) = small(hop_kernel, "hop", flags, [totals[k]] + arrived[k], dep, [(plain, BF16)])
                hop(k, dep)
            elif stage == hops:
                here[k], dep = small(
                    side_kernel, "side", flags, [mine[k], other[k]] + arrived[k], dep, [(plain, F32), (plain, BF16)]
                )
                there[k] = swap(dep, 2)
            elif stage == hops + 1:
                own, dep = small(
                    core_kernel, "core", flags, [keep[k], received[k], here[k], there[k]], dep, [((2,) + plain, F32)] * 2
                )
                states[k] = (own, swap(dep, 1))
            elif k < CHUNKS - 1:
                dep, sq = branch(place, query, gate_input, ag, ld, states[k], [o[k] for o in intra_outs], dep, k, hd)
                early.append(dep)
                squares.append(sq)
        dep = more_intra(dep)

    expert_count = EXP_DEV * size
    capacity = 5 * tok_rows * expert_ids.shape[1] // (4 * expert_count)
    outgoing = finish(
        place, query, gate_input, ag, ld, states[-1], [o[-1] for o in intra_outs], early, squares,
        residual, mg, expert_ids.T, dep, capacity, expert_count, hd,
    )
    return land(lax.all_to_all(outgoing, "ctx", split_axis=0, concat_axis=0, tiled=True))


def solution(mesh):
    rows = P(("groups", "ctx"), None)
    in_specs = (rows, rows, rows, rows, rows, rows, P(), P(), rows)
    out_specs = P(("groups", "ctx"), None, None)
    return jax.shard_map(body, mesh=mesh, in_specs=in_specs, out_specs=out_specs, check_vma=False)
```

```python
import functools
import jax
import jax.numpy as jnp
from jax import lax
from jax.experimental import pallas as pl
from jax.experimental.pallas import tpu as pltpu
from jax.sharding import PartitionSpec as P

EXP_DEV = 1
SLOTS = 4
CHUNKS = 2
LANES = 128
TAIL = 8
F32 = jnp.float32
BF16 = jnp.bfloat16
ANY = pl.BlockSpec(memory_space=pl.ANY)
VMEM = pl.BlockSpec(memory_space=pltpu.VMEM)
SMEM = pl.BlockSpec(memory_space=pltpu.SMEM)
BRIEF = pl.CostEstimate(flops=1, bytes_accessed=1, transcendentals=0)


def dot(a, b, contract=(1, 0)):
    return lax.dot_general(a, b, ((contract[:1], contract[1:]), ((), ())), preferred_element_type=F32)


def running(ld_ref, group, count):
    ld = ld_ref[:count, :]
    for g in range(1, ld_ref.shape[0] // count):
        ld = jnp.where(group == g, ld_ref[g * count : (g + 1) * count, :], ld)
    tok = ld.shape[1]
    row = lax.broadcasted_iota(jnp.int32, (tok, tok), 0)
    col = lax.broadcasted_iota(jnp.int32, (tok, tok), 1)
    upper = (row <= col).astype(F32).astype(BF16)
    high = ld.astype(BF16)
    rest = ld - high.astype(F32)
    mid = rest.astype(BF16)
    low = (rest - mid.astype(F32)).astype(BF16)
    return dot(high, upper) + (dot(mid, upper) + dot(low, upper))


def state_kernel(first_slot, chunk, hd, place, k_ref, v_ref, ld_ref, dep, out):
    per = out.shape[1]
    for j in range(2):
        group = jnp.bitwise_xor(j + first_slot, place[0])
        cum = running(ld_ref, group, per * CHUNKS)[chunk * per : (chunk + 1) * per]
        total = cum[:, -1:]
        weight = jnp.exp(total - cum)
        decay = jnp.exp(total)
        for i in range(per):
            cols = pl.ds(pl.multiple_of(((group * CHUNKS + chunk) * per + i) * hd, hd), hd)
            wk = (weight[i : i + 1, :] * k_ref[:, cols].T.astype(F32)).astype(BF16)
            out[j, i, :hd, :] = dot(wk, v_ref[:, cols])
            out[j, i, hd:, :] = jnp.broadcast_to(decay[i : i + 1, :], (TAIL, hd))


def block_states(place, key_rows, value_rows, log_decay, dep, first_slot, chunk, hd):
    per = key_rows.shape[1] // SLOTS // CHUNKS // hd
    return pl.pallas_call(
        functools.partial(state_kernel, first_slot, chunk, hd),
        in_specs=[SMEM] + [VMEM] * 3 + [ANY],
        out_specs=VMEM,
        out_shape=jax.ShapeDtypeStruct((2, per, hd + TAIL, hd), F32),
        compiler_params=pltpu.CompilerParams(vmem_limit_bytes=16 << 20),
        cost_estimate=BRIEF,
        name="block_states",
    )(place, key_rows, value_rows, log_decay, dep)


def intra_kernel(hd, slot, place, q_ref, k_ref, v_ref, ld_ref, dep, *outs):
    tok, cw = outs[0].shape
    per = cw // hd
    gh = per * CHUNKS
    half = tok // 2
    group = jnp.bitwise_xor(slot, place[0])
    cum_rows = running(ld_ref, group, gh)
    cum = cum_rows.T
    row = lax.broadcasted_iota(jnp.int32, (half, half), 0)
    col = lax.broadcasted_iota(jnp.int32, (half, half), 1)
    causal = row >= col
    for i in range(gh):
        cols = pl.ds(pl.multiple_of(group * (gh * hd) + i * hd, hd), hd)
        o_ref, to = outs[i // per], slice(i % per * hd, (i % per + 1) * hd)
        down, across = cum[:, i : i + 1], cum_rows[i : i + 1, :]
        q, k, v = q_ref[:, cols], k_ref[:, cols], v_ref[:, cols]
        parts = []
        for first in (0, half):
            at = slice(first, first + half)
            score = dot(q[at], k[at], (1, 1))
            weights = jnp.where(causal, score * jnp.exp(down[at] - across[:, at]), 0.0).astype(BF16)
            parts.append(dot(weights, v[at]))
        o_ref[:half, to] = parts[0]
        middle = across[:, half - 1 : half]
        score = dot(q[half:], k[:half], (1, 1))
        weights = (score * (jnp.exp(down[half:] - middle) * jnp.exp(middle - across[:, :half]))).astype(BF16)
        o_ref[half:, to] = parts[1] + dot(weights, v[:half])


def intra(place, query, key_rows, value_rows, log_decay, dep, slot, hd):
    tok, width = query.shape
    cw = width // SLOTS // CHUNKS
    return pl.pallas_call(
        functools.partial(intra_kernel, hd, slot),
        in_specs=[SMEM] + [VMEM] * 4 + [ANY],
        out_specs=[VMEM] * CHUNKS,
        out_shape=[jax.ShapeDtypeStruct((tok, cw), F32)] * CHUNKS,
        compiler_params=pltpu.CompilerParams(vmem_limit_bytes=16 << 20),
        cost_estimate=BRIEF,
        name="intra",
    )(place, query, key_rows, value_rows, log_decay, dep)


def add_branch(hd, chunk, place, q_ref, gate_ref, ag_ref, ld_ref, own, there, ins, o_ref):
    per = own.shape[1]
    cw = per * hd
    squares = 0.0
    for slot in range(SLOTS):
        group = jnp.bitwise_xor(slot, place[0])
        cum = running(ld_ref, group, per * CHUNKS)[chunk * per : (chunk + 1) * per]
        grow = jnp.exp(cum).T
        for i in range(per):
            carried = (own if slot < 2 else there)[slot % 2, i]
            high = carried.astype(BF16)
            low = (carried - high.astype(F32)).astype(BF16)
            where = pl.ds(pl.multiple_of((group * CHUNKS + chunk) * cw + i * hd, hd), hd)
            q = q_ref[:, where]
            att = ins[slot][:, i * hd : (i + 1) * hd] + grow[:, i : i + 1] * (dot(q, high) + dot(q, low))
            squares = squares + att * att
            opened = 0.5 * jnp.tanh(0.5 * gate_ref[:, where].astype(F32)) + 0.5
            o_ref[:, slot * cw + i * hd : slot * cw + (i + 1) * hd] = att * (ag_ref[:, where] * opened)
    return squares


def branch_kernel(hd, chunk, place, q_ref, gate_ref, ag_ref, ld_ref, own, there, dep, *rest):
    o_ref, sq_ref = rest[SLOTS:]
    sq_ref[...] = add_branch(
        hd, chunk, place, q_ref, gate_ref, ag_ref, ld_ref, own, there, rest[:SLOTS], o_ref
    )


def branch(place, query, gate, attn_gain, log_decay, states, intra_outs, dep, chunk, hd):
    tok, width = query.shape
    return pl.pallas_call(
        functools.partial(branch_kernel, hd, chunk),
        in_specs=[SMEM] + [VMEM] * 6 + [ANY] + [VMEM] * SLOTS,
        out_specs=[VMEM] * 2,
        out_shape=[
            jax.ShapeDtypeStruct((tok, width // CHUNKS), F32),
            jax.ShapeDtypeStruct((tok, hd), F32),
        ],
        compiler_params=pltpu.CompilerParams(vmem_limit_bytes=16 << 20),
        cost_estimate=BRIEF,
        name="branch",
    )(place, query, gate, attn_gain, log_decay, *states, dep, *intra_outs)


def finish_kernel(hd, cap, place, q_ref, gate_ref, ag_ref, ld_ref, own, there, dep, *rest):
    ins, rest = rest[:SLOTS], rest[SLOTS:]
    early, rest = rest[: CHUNKS - 1], rest[CHUNKS - 1 :]
    squares, rest = rest[: CHUNKS - 1], rest[CHUNKS - 1 :]
    res_ref, mg_ref, ids_ref, o_hbm, late, sq, hidden, normed, target, staged, sems = rest
    tok, width = normed.shape
    per = own.shape[1]
    cw = per * hd

    top = ids_ref.shape[0]
    experts = o_hbm.shape[0] // cap
    ids = ids_ref[...]
    expert = lax.broadcasted_iota(jnp.int32, (experts, tok), 0)
    hot = [(ids[k : k + 1, :] == expert).astype(F32) for k in range(top)]
    row = lax.broadcasted_iota(jnp.int32, (tok, tok), 0)
    col = lax.broadcasted_iota(jnp.int32, (tok, tok), 1)
    count = dot(sum(hot).astype(BF16), (row < col).astype(F32).astype(BF16))
    for k in range(top):
        slot = jnp.sum(hot[k] * count, axis=0, keepdims=True).astype(jnp.int32)
        target[k : k + 1, :] = ids[k : k + 1, :] * cap + slot
        count = count + hot[k]

    part = add_branch(
        hd, CHUNKS - 1, place, q_ref, gate_ref, ag_ref, ld_ref, own, there, ins, late
    )
    for s in squares:
        part = part + s[...]
    sq[...] = part

    rows = hidden.shape[0]

    @pl.loop(0, tok // rows)
    def _(step):
        at = pl.ds(pl.multiple_of(step * rows, rows), rows)
        scale = lax.rsqrt(jnp.sum(sq[at, :], axis=-1, keepdims=True) / width + 1e-06)
        total = jnp.zeros((rows, LANES), F32)
        for slot in range(SLOTS):
            group = jnp.bitwise_xor(slot, place[0])
            for k in range(CHUNKS):
                for n in range(cw // LANES):
                    here = slice(slot * cw + n * LANES, slot * cw + (n + 1) * LANES)
                    where = pl.ds(pl.multiple_of((group * CHUNKS + k) * cw + n * LANES, LANES), LANES)
                    value = (early[k] if k < CHUNKS - 1 else late)[at, here]
                    value = res_ref[at, where].astype(F32) + value * scale
                    total = total + value * value
                    hidden[:, where] = value
        scale = lax.rsqrt(jnp.sum(total, axis=-1, keepdims=True) / width + 1e-06)
        for n in range(width // LANES):
            cols = slice(n * LANES, (n + 1) * LANES)
            normed[at, cols] = (hidden[:, cols] * scale * mg_ref[:, cols]).astype(BF16)

    steps = sems.shape[0]
    out_rows = o_hbm.shape[0] // steps

    def copy(step):
        at = pl.ds(pl.multiple_of(step * out_rows, out_rows), out_rows)
        return pltpu.make_async_copy(staged.at[at], o_hbm.at[at], sems.at[step])

    @pl.loop(0, steps)
    def _(step):
        at = pl.ds(pl.multiple_of(step * out_rows, out_rows), out_rows)
        row = lax.broadcasted_iota(jnp.int32, (out_rows, tok), 0) + step * out_rows
        hit = row == target[0:1, :]
        for k in range(1, top):
            hit = hit | (row == target[k : k + 1, :])
        pick = hit.astype(F32).astype(BF16)
        part = width // 4
        for n in range(4):
            cols = slice(n * part, (n + 1) * part)
            staged[at, cols] = dot(pick, normed[:, cols]).astype(BF16)
        copy(step).start()

    for step in range(steps):
        copy(step).wait()


def finish(
    place, query, gate, attn_gain, log_decay, states, intra_outs, early, squares, residual, moe_gain, ids, dep, cap, experts, hd
):
    tok, width = query.shape
    steps = 4
    return pl.pallas_call(
        functools.partial(finish_kernel, hd, cap),
        in_specs=[SMEM] + [VMEM] * 6 + [ANY] + [VMEM] * (SLOTS + 2 * (CHUNKS - 1) + 3),
        out_specs=pl.BlockSpec(memory_space=pl.ANY),
        scratch_shapes=[
            pltpu.VMEM((tok, width // CHUNKS), F32),
            pltpu.VMEM((tok, hd), F32),
            pltpu.VMEM((tok // 4, width), F32),
            pltpu.VMEM((tok, width), BF16),
            pltpu.VMEM((8, tok), jnp.int32),
            pltpu.VMEM((experts * cap, width), BF16),
            pltpu.SemaphoreType.DMA((steps,)),
        ],
        out_shape=jax.ShapeDtypeStruct((experts * cap, width), BF16),
        compiler_params=pltpu.CompilerParams(vmem_limit_bytes=24 << 20),
        cost_estimate=BRIEF,
        name="finish",
    )(place, query, gate, attn_gain, log_decay, *states, dep, *intra_outs, *early, *squares, residual, moe_gain, ids)


def land_kernel(i_ref, o_ref, sems):
    steps = sems.shape[0]
    rows = i_ref.shape[0] // steps
    copies = [
        pltpu.make_async_copy(
            i_ref.at[pl.ds(n * rows, rows)], o_ref.at[0, pl.ds(n * rows, rows)], sems.at[n]
        )
        for n in range(steps)
    ]
    for c in copies:
        c.start()
    for c in copies:
        c.wait()


def land(arrived):
    return pl.pallas_call(
        land_kernel,
        in_specs=[ANY],
        out_specs=ANY,
        scratch_shapes=[pltpu.SemaphoreType.DMA((8,))],
        out_shape=jax.ShapeDtypeStruct((1,) + arrived.shape, arrived.dtype),
        compiler_params=pltpu.CompilerParams(vmem_limit_bytes=16 << 20),
        cost_estimate=BRIEF,
        name="land",
    )(arrived)


def swap(value, bit):
    size = lax.axis_size("ctx")
    return lax.ppermute(value, "ctx", [(i, i ^ bit) for i in range(size)])


def small(kernel, name, flags, ins, dep, outs):
    return pl.pallas_call(
        kernel,
        in_specs=[SMEM] + [VMEM] * len(ins) + [ANY],
        out_specs=[VMEM] * len(outs),
        out_shape=[jax.ShapeDtypeStruct(shape, kind) for shape, kind in outs],
        compiler_params=pltpu.CompilerParams(vmem_limit_bytes=16 << 20),
        cost_estimate=BRIEF,
        name=name,
    )(flags, *ins, dep)


def later(before, decay, state):
    return decay * before + state


def decay_rows(decay, rows):
    high = decay.astype(BF16).astype(F32)
    mid = (decay - high).astype(BF16).astype(F32)
    low = decay - high - mid
    row = lax.broadcasted_iota(jnp.int32, (decay.shape[0], rows, decay.shape[2]), 1)
    return jnp.where(row == 0, high, jnp.where(row == 1, mid, jnp.where(row == 2, low, 0.0)))


def chip_kernel(flags, keep, received, dep, mine, sent, rest):
    hd = keep.shape[-1]
    low = flags[1] == 0
    for slot in range(2):
        a = jnp.where(low, keep[slot], received[slot])
        b = jnp.where(low, received[slot], keep[slot])
        state = later(a[:, :hd, :], b[:, hd : hd + 1, :], b[:, :hd, :])
        decay = a[:, hd:, :] * b[:, hd:, :]
        if slot == 0:
            mine[:, :hd, :] = state
            mine[:, hd:, :] = decay
        else:
            high = state.astype(BF16)
            sent[:, :hd, :] = high
            sent[:, hd:, :] = decay_rows(decay[:, :1, :], 2 * TAIL).astype(BF16)
            rest[...] = (state - high.astype(F32)).astype(BF16)


def late_kernel(flags, *refs):
    count = len(refs) // 2
    for i_ref, o_ref in zip(refs[:count], refs[count + 1 :]):
        o_ref[...] = i_ref[...]


def row_parts(flags, mine, other, rest=None):
    hd = mine.shape[-1]
    low = flags[2] == 0
    a = (mine[:, :hd, :], mine[:, hd : hd + 1, :])
    state = other[:, :hd, :].astype(F32)
    if rest is not None:
        state = state + rest[...].astype(F32)
    b = (state, jnp.sum(other[:, hd:, :].astype(F32), axis=1, keepdims=True))
    first = tuple(jnp.where(low, x, y) for x, y in zip(a, b))
    second = tuple(jnp.where(low, y, x) for x, y in zip(a, b))
    return first, second


def row_kernel(flags, mine, other, dep, sent):
    first, second = row_parts(flags, mine, other)
    sent[...] = later(first[0], second[1], second[0]).astype(sent.dtype)


def arrived_sum(refs):
    return sum(r[...].astype(F32) for r in refs)


def hop_kernel(flags, mine, other, rest, *more):
    hops, sent = more[:-2], more[-1]
    first, second = row_parts(flags, mine, other, rest)
    total = later(first[0], second[1], second[0])
    sent[...] = later(arrived_sum(hops), first[1] * second[1], total).astype(sent.dtype)


def side_kernel(flags, mine, other, rest, *more):
    hops, (_, here, sent) = more[:-3], more[-3:]
    low = flags[2] == 0
    first, _ = row_parts(flags, mine, other, rest)
    before = arrived_sum(hops)
    entered = later(before, first[1], first[0])
    here[...] = jnp.where(low, before, entered)
    sent[...] = jnp.where(low, entered, before).astype(sent.dtype)


def core_kernel(flags, keep, received, here, there, dep, own, sent):
    hd = keep.shape[-1]
    low = flags[1] == 0
    for slot, ref in ((0, here), (1, there)):
        pair = ref[...].astype(F32)
        first = jnp.where(low, keep[slot], received[slot])
        second = later(pair, first[:, hd : hd + 1, :], first[:, :hd, :])
        own[slot] = jnp.where(low, pair, second)
        sent[slot] = jnp.where(low, second, pair)


def body(
    query, key_rows, value_rows, log_decay, gate_input, residual, attn_gain, moe_gain, expert_ids
):
    tok_rows, model_width = query.shape
    heads = log_decay.shape[1]
    hd = model_width // heads
    per = heads // SLOTS // CHUNKS
    size = lax.axis_size("ctx")
    hops = size // SLOTS - 1
    index = lax.axis_index("ctx").astype(jnp.int32)
    core, side = jnp.bitwise_and(index, 1), jnp.bitwise_and(lax.shift_right_logical(index, 1), 1)
    place = (2 * core + side)[None]
    flags = jnp.stack([2 * core + side, core, side])
    ld = log_decay.T
    ag, mg = attn_gain[None], moe_gain[None]
    full, wire, plain = (per, hd + TAIL, hd), (per, hd + 2 * TAIL, hd), (per, hd, hd)

    received, keep, mine, other, rest = [], [], [], [], []
    dep = ld

    def chip(k, dep):
        m, t, r = small(
            chip_kernel, "chip", flags, [keep[k], received[k]], dep, [(full, F32), (wire, BF16), (plain, BF16)]
        )
        mine.append(m)
        other.append(swap(t, 2))
        rest.append(r)
        return m

    for k in range(CHUNKS):
        dep = block_states(place, key_rows, value_rows, ld, dep, 2, k, hd)
        received.append(swap(dep, 1))
        if k:
            dep = chip(k - 1, dep)
        dep = block_states(place, key_rows, value_rows, ld, dep, 0, k, hd)
        keep.append(dep)
    dep = chip(CHUNKS - 1, dep)

    intra_outs = []
    arrived = [[] for _ in range(CHUNKS)]
    here, there, states = [None] * CHUNKS, [None] * CHUNKS, [None] * CHUNKS
    early, squares = [], []

    def more_intra(dep):
        if len(intra_outs) < SLOTS:
            intra_outs.append(intra(place, query, key_rows, value_rows, ld, dep, len(intra_outs), hd))
            dep = intra_outs[-1][0]
        return dep

    def hop(k, sent):
        s = len(arrived[k])
        pairs = [(s * SLOTS + j, (s + 1) * SLOTS + j) for j in range(SLOTS)]
        arrived[k].append(lax.ppermute(sent, "ctx", pairs))

    dep = more_intra(dep)
    rest = small(late_kernel, "late", flags, rest, dep, [(plain, BF16)] * CHUNKS)
    dep = rest[0]
    rest = [swap(r, 2) for r in rest]
    order = sorted(((k, stage) for k in range(CHUNKS) for stage in range(hops + 2)), key=lambda r: r[1] + 0.6 * r[0])
    for k, stage in order:
        if stage == 0:
            (dep,) = small(row_kernel, "row", flags, [mine[k], other[k]], dep, [(plain, BF16)])
            hop(k, dep)
        elif stage < hops:
            (dep,) = small(
                hop_kernel, "hop", flags, [mine[k], other[k], rest[k]] + arrived[k], dep, [(plain, BF16)]
            )
            hop(k, dep)
        elif stage == hops:
            here[k], dep = small(
                side_kernel,
                "side",
                flags,
                [mine[k], other[k], rest[k]] + arrived[k],
                dep,
                [(plain, F32), (plain, BF16)],
            )
            there[k] = swap(dep, 2)
        else:
            own, dep = small(
                core_kernel, "core", flags, [keep[k], received[k], here[k], there[k]], dep, [((2,) + plain, F32)] * 2
            )
            states[k] = (own, swap(dep, 1))
        dep = more_intra(dep)
    while len(intra_outs) < SLOTS:
        dep = more_intra(dep)
    for k in range(CHUNKS - 1):
        dep, sq = branch(place, query, gate_input, ag, ld, states[k], [o[k] for o in intra_outs], dep, k, hd)
        early.append(dep)
        squares.append(sq)

    expert_count = EXP_DEV * size
    capacity = 5 * tok_rows * expert_ids.shape[1] // (4 * expert_count)
    outgoing = finish(
        place, query, gate_input, ag, ld, states[-1], [o[-1] for o in intra_outs], early, squares,
        residual, mg, expert_ids.T, dep, capacity, expert_count, hd,
    )
    return land(lax.all_to_all(outgoing, "ctx", split_axis=0, concat_axis=0, tiled=True))


def solution(mesh):
    rows = P(("groups", "ctx"), None)
    in_specs = (rows, rows, rows, rows, rows, rows, P(), P(), rows)
    out_specs = P(("groups", "ctx"), None, None)
    return jax.shard_map(body, mesh=mesh, in_specs=in_specs, out_specs=out_specs, check_vma=False)
```

```python
import functools
import jax
import jax.numpy as jnp
from jax import lax
from jax.experimental import pallas as pl
from jax.experimental.pallas import tpu as pltpu
from jax.sharding import PartitionSpec as P

EXP_DEV = 1
SLOTS = 4
CHUNKS = 2
LANES = 128
TAIL = 8
F32 = jnp.float32
BF16 = jnp.bfloat16
ANY = pl.BlockSpec(memory_space=pl.ANY)
VMEM = pl.BlockSpec(memory_space=pltpu.VMEM)
SMEM = pl.BlockSpec(memory_space=pltpu.SMEM)
BRIEF = pl.CostEstimate(flops=1, bytes_accessed=1, transcendentals=0)


def dot(a, b, contract=(1, 0)):
    return lax.dot_general(a, b, ((contract[:1], contract[1:]), ((), ())), preferred_element_type=F32)


def running(ld):
    tok = ld.shape[1]
    row = lax.broadcasted_iota(jnp.int32, (tok, tok), 0)
    col = lax.broadcasted_iota(jnp.int32, (tok, tok), 1)
    upper = (row <= col).astype(F32).astype(BF16)
    high = ld.astype(BF16)
    rest = ld - high.astype(F32)
    mid = rest.astype(BF16)
    low = (rest - mid.astype(F32)).astype(BF16)
    return dot(high, upper) + (dot(mid, upper) + dot(low, upper))


def start_kernel(cap, experts, ld_ref, ids_ref, dep, cum_ref, target_ref):
    cum_ref[...] = running(ld_ref[...])
    top, tok = ids_ref.shape
    ids = ids_ref[...]
    expert = lax.broadcasted_iota(jnp.int32, (experts, tok), 0)
    hot = [(ids[k : k + 1, :] == expert).astype(F32) for k in range(top)]
    row = lax.broadcasted_iota(jnp.int32, (tok, tok), 0)
    col = lax.broadcasted_iota(jnp.int32, (tok, tok), 1)
    count = dot(sum(hot).astype(BF16), (row < col).astype(F32).astype(BF16))
    for k in range(top):
        slot = jnp.sum(hot[k] * count, axis=0, keepdims=True).astype(jnp.int32)
        target_ref[k : k + 1, :] = ids[k : k + 1, :] * cap + slot
        count = count + hot[k]


def start(log_decay, ids, dep, cap, experts):
    return pl.pallas_call(
        functools.partial(start_kernel, cap, experts),
        in_specs=[VMEM] * 2 + [ANY],
        out_specs=[VMEM] * 2,
        out_shape=[jax.ShapeDtypeStruct(a.shape, a.dtype) for a in (log_decay, ids)],
        compiler_params=pltpu.CompilerParams(vmem_limit_bytes=16 << 20),
        cost_estimate=BRIEF,
        name="start",
    )(log_decay, ids, dep)


def group_rows(cum, group, first, count):
    size = cum.shape[0] // SLOTS
    rows = cum[first : first + count]
    for g in range(1, SLOTS):
        rows = jnp.where(group == g, cum[g * size + first : g * size + first + count], rows)
    return rows


def state_kernel(first_slot, chunk, hd, place, k_ref, v_ref, ld_ref, dep, out):
    per = out.shape[1]
    cum = running(ld_ref[...])
    for j in range(2):
        group = jnp.bitwise_xor(j + first_slot, place[0])
        rows = group_rows(cum, group, chunk * per, per)
        total = rows[:, -1:]
        weight = jnp.exp(total - rows)
        decay = jnp.exp(total)
        for i in range(per):
            cols = pl.ds(pl.multiple_of(((group * CHUNKS + chunk) * per + i) * hd, hd), hd)
            wk = (weight[i : i + 1, :] * k_ref[:, cols].T.astype(F32)).astype(BF16)
            out[j, i, :hd, :] = dot(wk, v_ref[:, cols])
            out[j, i, hd:, :] = jnp.broadcast_to(decay[i : i + 1, :], (TAIL, hd))


def block_states(place, key_rows, value_rows, log_decay, dep, first_slot, chunk, hd):
    per = key_rows.shape[1] // SLOTS // CHUNKS // hd
    return pl.pallas_call(
        functools.partial(state_kernel, first_slot, chunk, hd),
        in_specs=[SMEM] + [VMEM] * 3 + [ANY],
        out_specs=VMEM,
        out_shape=jax.ShapeDtypeStruct((2, per, hd + TAIL, hd), F32),
        compiler_params=pltpu.CompilerParams(vmem_limit_bytes=16 << 20),
        cost_estimate=BRIEF,
        name="block_states",
    )(place, key_rows, value_rows, log_decay, dep)


def intra_kernel(hd, slot, place, q_ref, k_ref, v_ref, cum_ref, dep, *outs):
    tok, cw = outs[0].shape
    per = cw // hd
    gh = per * CHUNKS
    half = tok // 2
    group = jnp.bitwise_xor(slot, place[0])
    cum_rows = group_rows(cum_ref[...], group, 0, gh)
    cum = cum_rows.T
    row = lax.broadcasted_iota(jnp.int32, (half, half), 0)
    col = lax.broadcasted_iota(jnp.int32, (half, half), 1)
    causal = row >= col
    for i in range(gh):
        cols = pl.ds(pl.multiple_of(group * (gh * hd) + i * hd, hd), hd)
        o_ref, to = outs[i // per], slice(i % per * hd, (i % per + 1) * hd)
        down, across = cum[:, i : i + 1], cum_rows[i : i + 1, :]
        q, k, v = q_ref[:, cols], k_ref[:, cols], v_ref[:, cols]
        score = dot(q, k, (1, 1))
        diagonal = []
        for first in (0, half):
            at = slice(first, first + half)
            diagonal.append(jnp.where(causal, score[at, at] * jnp.exp(down[at] - across[:, at]), 0.0).astype(BF16))
        middle = across[:, half - 1 : half]
        below = score[half:, :half] * (jnp.exp(down[half:] - middle) * jnp.exp(middle - across[:, :half]))
        weights = jnp.concatenate(
            [
                jnp.concatenate([diagonal[0], jnp.zeros((half, half), BF16)], axis=1),
                jnp.concatenate([below.astype(BF16), diagonal[1]], axis=1),
            ],
            axis=0,
        )
        o_ref[:, to] = dot(weights, v)


def intra(place, query, key_rows, value_rows, cum, dep, slot, hd):
    tok, width = query.shape
    cw = width // SLOTS // CHUNKS
    return pl.pallas_call(
        functools.partial(intra_kernel, hd, slot),
        in_specs=[SMEM] + [VMEM] * 4 + [ANY],
        out_specs=[VMEM] * CHUNKS,
        out_shape=[jax.ShapeDtypeStruct((tok, cw), F32)] * CHUNKS,
        compiler_params=pltpu.CompilerParams(vmem_limit_bytes=16 << 20),
        cost_estimate=BRIEF,
        name="intra",
    )(place, query, key_rows, value_rows, cum, dep)


def add_branch(hd, chunk, slots, place, q_ref, gate_ref, ag_ref, cum_ref, states, ins, o_ref):
    per = states[0].shape[1]
    cw = per * hd
    squares = 0.0
    grown = jnp.exp(cum_ref[...])
    for n, slot in enumerate(slots):
        group = jnp.bitwise_xor(slot, place[0])
        grow = group_rows(grown, group, chunk * per, per).T
        for i in range(per):
            carried = states[n // 2][slot % 2, i]
            high = carried.astype(BF16)
            low = (carried - high.astype(F32)).astype(BF16)
            where = pl.ds(pl.multiple_of((group * CHUNKS + chunk) * cw + i * hd, hd), hd)
            q = q_ref[:, where]
            att = ins[n][:, i * hd : (i + 1) * hd] + grow[:, i : i + 1] * (dot(q, high) + dot(q, low))
            squares = squares + att * att
            opened = 0.5 * jnp.tanh(0.5 * gate_ref[:, where].astype(F32)) + 0.5
            o_ref[:, n * cw + i * hd : n * cw + (i + 1) * hd] = att * (ag_ref[:, where] * opened)
    return squares


def branch_kernel(hd, chunk, slots, place, q_ref, gate_ref, ag_ref, cum_ref, state, dep, *rest):
    o_ref, sq_ref = rest[-2:]
    sq_ref[...] = add_branch(
        hd, chunk, slots, place, q_ref, gate_ref, ag_ref, cum_ref, (state,), rest[:-2], o_ref
    )


def branch(place, query, gate, attn_gain, cum, states, intra_outs, dep, chunk, side, hd):
    tok, width = query.shape
    slots = (2 * side, 2 * side + 1)
    return pl.pallas_call(
        functools.partial(branch_kernel, hd, chunk, slots),
        in_specs=[SMEM] + [VMEM] * 5 + [ANY] + [VMEM] * 2,
        out_specs=[VMEM] * 2,
        out_shape=[
            jax.ShapeDtypeStruct((tok, 2 * (width // SLOTS // CHUNKS)), F32),
            jax.ShapeDtypeStruct((tok, hd), F32),
        ],
        compiler_params=pltpu.CompilerParams(vmem_limit_bytes=16 << 20),
        cost_estimate=BRIEF,
        name="branch",
    )(place, query, gate, attn_gain, cum, states[side], dep, *[intra_outs[j][chunk] for j in slots])


def finish_kernel(hd, place, q_ref, gate_ref, ag_ref, cum_ref, there, dep, *rest):
    ins, rest = rest[:2], rest[2:]
    count = 2 * CHUNKS - 1
    early, squares, rest = rest[:count], rest[count : 2 * count], rest[2 * count :]
    res_ref, mg_ref, target, o_hbm, late, sq, sums, hidden, normed, pick, staged, sems = rest
    tok, width = normed.shape
    per = there.shape[1]
    cw = per * hd
    top = target.shape[0]

    part = add_branch(
        hd, CHUNKS - 1, (2, 3), place, q_ref, gate_ref, ag_ref, cum_ref, (there,), ins, late
    )
    for s in squares:
        part = part + s[...]
    rows = tok // 4
    scale = lax.rsqrt(jnp.sum(part, axis=-1, keepdims=True) / width + 1e-06)
    sq[...] = jnp.broadcast_to(scale, sq.shape)

    @pl.loop(0, tok // rows)
    def _(step):
        at = pl.ds(pl.multiple_of(step * rows, rows), rows)
        scale = sq[at, :]
        total = jnp.zeros((rows, LANES), F32)
        for slot in range(SLOTS):
            group = jnp.bitwise_xor(slot, place[0])
            for k in range(CHUNKS):
                for n in range(cw // LANES):
                    source = (*early, late)[2 * k + slot // 2]
                    here = slice(slot % 2 * cw + n * LANES, slot % 2 * cw + (n + 1) * LANES)
                    where = pl.ds(pl.multiple_of((group * CHUNKS + k) * cw + n * LANES, LANES), LANES)
                    value = source[at, here]
                    value = res_ref[at, where].astype(F32) + value * scale
                    total = total + value * value
                    hidden[at, where] = value
        sums[at, :] = total

    scale = lax.rsqrt(jnp.sum(sums[...], axis=-1, keepdims=True) / width + 1e-06)
    sq[...] = jnp.broadcast_to(scale, sq.shape)

    @pl.loop(0, tok // rows)
    def _(step):
        at = pl.ds(pl.multiple_of(step * rows, rows), rows)
        scale = sq[at, :]
        for n in range(width // LANES):
            cols = slice(n * LANES, (n + 1) * LANES)
            normed[at, cols] = (hidden[at, cols] * scale * mg_ref[:, cols]).astype(BF16)

    row = lax.broadcasted_iota(jnp.int32, (o_hbm.shape[0], tok), 0)
    hit = row == target[0:1, :]
    for k in range(1, top):
        hit = hit | (row == target[k : k + 1, :])
    pick[...] = hit.astype(F32).astype(BF16)
    steps = sems.shape[0]
    block = width // steps
    copies = []
    for step in range(steps):
        for n in range(step * block, (step + 1) * block, 2 * LANES):
            cols = slice(n, n + 2 * LANES)
            staged[:, cols] = dot(pick[...], normed[:, cols]).astype(BF16)
        cols = pl.ds(step * block, block)
        copies.append(pltpu.make_async_copy(staged.at[:, cols], o_hbm.at[:, cols], sems.at[step]))
        copies[-1].start()
    for c in copies:
        c.wait()


def finish(place, query, gate, attn_gain, cum, there, intra_outs, early, squares, residual, moe_gain, target, dep, rows, hd):
    tok, width = query.shape
    steps = 4
    return pl.pallas_call(
        functools.partial(finish_kernel, hd),
        in_specs=[SMEM] + [VMEM] * 5 + [ANY] + [VMEM] * (2 + 2 * (2 * CHUNKS - 1) + 3),
        out_specs=pl.BlockSpec(memory_space=pl.ANY),
        scratch_shapes=[
            pltpu.VMEM((tok, width // CHUNKS // 2), F32),
            pltpu.VMEM((tok, LANES), F32),
            pltpu.VMEM((tok, LANES), F32),
            pltpu.VMEM((tok, width), F32),
            pltpu.VMEM((tok, width), BF16),
            pltpu.VMEM((rows, tok), BF16),
            pltpu.VMEM((rows, width), BF16),
            pltpu.SemaphoreType.DMA((steps,)),
        ],
        out_shape=jax.ShapeDtypeStruct((rows, width), BF16),
        compiler_params=pltpu.CompilerParams(vmem_limit_bytes=28 << 20),
        cost_estimate=BRIEF,
        name="finish",
    )(
        place, query, gate, attn_gain, cum, there, dep, *[o[-1] for o in intra_outs[2:]],
        *early, *squares, residual, moe_gain, target,
    )


def land_kernel(i_ref, o_ref, sems):
    steps = sems.shape[0]
    rows = i_ref.shape[0] // steps
    copies = [
        pltpu.make_async_copy(
            i_ref.at[pl.ds(n * rows, rows)], o_ref.at[0, pl.ds(n * rows, rows)], sems.at[n]
        )
        for n in range(steps)
    ]
    for c in copies:
        c.start()
    for c in copies:
        c.wait()


def land(arrived):
    return pl.pallas_call(
        land_kernel,
        in_specs=[ANY],
        out_specs=ANY,
        scratch_shapes=[pltpu.SemaphoreType.DMA((8,))],
        out_shape=jax.ShapeDtypeStruct((1,) + arrived.shape, arrived.dtype),
        compiler_params=pltpu.CompilerParams(vmem_limit_bytes=16 << 20),
        cost_estimate=BRIEF,
        name="land",
    )(arrived)


def swap(value, bit):
    size = lax.axis_size("ctx")
    return lax.ppermute(value, "ctx", [(i, i ^ bit) for i in range(size)])


def small(kernel, name, flags, ins, dep, outs):
    return pl.pallas_call(
        kernel,
        in_specs=[SMEM] + [VMEM] * len(ins) + [ANY],
        out_specs=[VMEM] * len(outs),
        out_shape=[jax.ShapeDtypeStruct(shape, kind) for shape, kind in outs],
        compiler_params=pltpu.CompilerParams(vmem_limit_bytes=16 << 20),
        cost_estimate=BRIEF,
        name=name,
    )(flags, *ins, dep)


def later(before, decay, state):
    return decay * before + state


def decay_rows(decay, rows):
    high = decay.astype(BF16).astype(F32)
    mid = (decay - high).astype(BF16).astype(F32)
    low = decay - high - mid
    row = lax.broadcasted_iota(jnp.int32, (decay.shape[0], rows, decay.shape[2]), 1)
    return jnp.where(row == 0, high, jnp.where(row == 1, mid, jnp.where(row == 2, low, 0.0)))


def chip_kernel(flags, keep, received, dep, mine, sent, rest):
    hd = keep.shape[-1]
    low = flags[1] == 0
    for slot in range(2):
        a = jnp.where(low, keep[slot], received[slot])
        b = jnp.where(low, received[slot], keep[slot])
        state = later(a[:, :hd, :], b[:, hd : hd + 1, :], b[:, :hd, :])
        decay = a[:, hd:, :] * b[:, hd:, :]
        if slot == 0:
            mine[:, :hd, :] = state
            mine[:, hd:, :] = decay
        else:
            high = state.astype(BF16)
            sent[:, :hd, :] = high
            sent[:, hd:, :] = decay_rows(decay[:, :1, :], 2 * TAIL).astype(BF16)
            rest[...] = (state - high.astype(F32)).astype(BF16)


def late_kernel(flags, *refs):
    count = len(refs) // 2
    for i_ref, o_ref in zip(refs[:count], refs[count + 1 :]):
        o_ref[...] = i_ref[...]


def row_parts(flags, mine, other, rest=None):
    hd = mine.shape[-1]
    low = flags[2] == 0
    a = (mine[:, :hd, :], mine[:, hd : hd + 1, :])
    state = other[:, :hd, :].astype(F32)
    if rest is not None:
        state = state + rest[...].astype(F32)
    b = (state, jnp.sum(other[:, hd:, :].astype(F32), axis=1, keepdims=True))
    first = tuple(jnp.where(low, x, y) for x, y in zip(a, b))
    second = tuple(jnp.where(low, y, x) for x, y in zip(a, b))
    return first, second


def row_kernel(flags, mine, other, dep, sent):
    first, second = row_parts(flags, mine, other)
    sent[...] = later(first[0], second[1], second[0]).astype(sent.dtype)


def arrived_sum(refs):
    return sum(r[...].astype(F32) for r in refs)


def hop_kernel(flags, mine, other, rest, *more):
    hops, sent = more[:-2], more[-1]
    first, second = row_parts(flags, mine, other, rest)
    total = later(first[0], second[1], second[0])
    sent[...] = later(arrived_sum(hops), first[1] * second[1], total).astype(sent.dtype)


def side_kernel(flags, mine, other, rest, *more):
    hops, (_, here, sent) = more[:-3], more[-3:]
    low = flags[2] == 0
    first, _ = row_parts(flags, mine, other, rest)
    before = arrived_sum(hops)
    entered = later(before, first[1], first[0])
    here[...] = jnp.where(low, before, entered)
    sent[...] = jnp.where(low, entered, before).astype(sent.dtype)


def core_kernel(flags, keep, received, here, there, dep, own, sent):
    hd = keep.shape[-1]
    low = flags[1] == 0
    for slot, ref in ((0, here), (1, there)):
        pair = ref[...].astype(F32)
        first = jnp.where(low, keep[slot], received[slot])
        second = later(pair, first[:, hd : hd + 1, :], first[:, :hd, :])
        own[slot] = jnp.where(low, pair, second)
        sent[slot] = jnp.where(low, second, pair)


def body(
    query, key_rows, value_rows, log_decay, gate_input, residual, attn_gain, moe_gain, expert_ids
):
    tok_rows, model_width = query.shape
    heads = log_decay.shape[1]
    hd = model_width // heads
    per = heads // SLOTS // CHUNKS
    size = lax.axis_size("ctx")
    hops = size // SLOTS - 1
    index = lax.axis_index("ctx").astype(jnp.int32)
    core, side = jnp.bitwise_and(index, 1), jnp.bitwise_and(lax.shift_right_logical(index, 1), 1)
    place = (2 * core + side)[None]
    flags = jnp.stack([2 * core + side, core, side])
    expert_count = EXP_DEV * size
    capacity = 5 * tok_rows * expert_ids.shape[1] // (4 * expert_count)
    ld = log_decay.T
    ag, mg = attn_gain[None], moe_gain[None]
    full, wire, plain = (per, hd + TAIL, hd), (per, hd + 2 * TAIL, hd), (per, hd, hd)

    received, keep, mine, other, rest = [], [], [], [], []
    dep = ld

    def chip(k, dep):
        m, t, r = small(
            chip_kernel, "chip", flags, [keep[k], received[k]], dep, [(full, F32), (wire, BF16), (plain, BF16)]
        )
        mine.append(m)
        other.append(swap(t, 2))
        rest.append(r)
        return m

    for k in range(CHUNKS):
        dep = block_states(place, key_rows, value_rows, ld, dep, 2, k, hd)
        received.append(swap(dep, 1))
        if k == 1:
            cum, target = start(ld, expert_ids.T, dep, capacity, expert_count)
            dep = cum
        if k:
            dep = chip(k - 1, dep)
        dep = block_states(place, key_rows, value_rows, ld, dep, 0, k, hd)
        keep.append(dep)
    dep = chip(CHUNKS - 1, dep)

    intra_outs = []
    arrived = [[] for _ in range(CHUNKS)]
    here, there, states = [None] * CHUNKS, [None] * CHUNKS, [None] * CHUNKS
    early, squares = [], []

    def more_intra(dep):
        if len(intra_outs) < SLOTS:
            intra_outs.append(intra(place, query, key_rows, value_rows, cum, dep, len(intra_outs), hd))
            dep = intra_outs[-1][0]
        return dep

    def hop(k, sent):
        s = len(arrived[k])
        pairs = [(s * SLOTS + j, (s + 1) * SLOTS + j) for j in range(SLOTS)]
        arrived[k].append(lax.ppermute(sent, "ctx", pairs))

    dep = more_intra(dep)
    rest = small(late_kernel, "late", flags, rest, dep, [(plain, BF16)] * CHUNKS)
    dep = rest[0]
    rest = [swap(r, 2) for r in rest]
    order = sorted(((k, stage) for k in range(CHUNKS) for stage in range(hops + 2)), key=lambda r: r[1] + 0.6 * r[0])
    for k, stage in order:
        if stage == 0:
            (dep,) = small(row_kernel, "row", flags, [mine[k], other[k]], dep, [(plain, BF16)])
            hop(k, dep)
        elif stage < hops:
            (dep,) = small(
                hop_kernel, "hop", flags, [mine[k], other[k], rest[k]] + arrived[k], dep, [(plain, BF16)]
            )
            hop(k, dep)
        elif stage == hops:
            here[k], dep = small(
                side_kernel,
                "side",
                flags,
                [mine[k], other[k], rest[k]] + arrived[k],
                dep,
                [(plain, F32), (plain, BF16)],
            )
            there[k] = swap(dep, 2)
        else:
            own, dep = small(
                core_kernel, "core", flags, [keep[k], received[k], here[k], there[k]], dep, [((2,) + plain, F32)] * 2
            )
            states[k] = (own, swap(dep, 1))
            for chunk, half in ((k - 1, 1), (k, 0)):
                if chunk >= 0:
                    dep, sq = branch(place, query, gate_input, ag, cum, states[chunk], intra_outs, dep, chunk, half, hd)
                    early.append(dep)
                    squares.append(sq)
        dep = more_intra(dep)
    outgoing = finish(
        place, query, gate_input, ag, cum, states[-1][1], intra_outs, early, squares,
        residual, mg, target, dep, expert_count * capacity, hd,
    )
    return land(lax.all_to_all(outgoing, "ctx", split_axis=0, concat_axis=0, tiled=True))


def solution(mesh):
    rows = P(("groups", "ctx"), None)
    in_specs = (rows, rows, rows, rows, rows, rows, P(), P(), rows)
    out_specs = P(("groups", "ctx"), None, None)
    return jax.shard_map(body, mesh=mesh, in_specs=in_specs, out_specs=out_specs, check_vma=False)
```

```python
import functools
import jax
import jax.numpy as jnp
from jax import lax
from jax.experimental import pallas as pl
from jax.experimental.pallas import tpu as pltpu
from jax.sharding import PartitionSpec as P

EXP_DEV = 1
SLOTS = 4
CHUNKS = 2
LANES = 128
TAIL = 8
F32 = jnp.float32
BF16 = jnp.bfloat16
ANY = pl.BlockSpec(memory_space=pl.ANY)
VMEM = pl.BlockSpec(memory_space=pltpu.VMEM)
SMEM = pl.BlockSpec(memory_space=pltpu.SMEM)
BRIEF = pl.CostEstimate(flops=1, bytes_accessed=1, transcendentals=0)


def dot(a, b, contract=(1, 0)):
    return lax.dot_general(a, b, ((contract[:1], contract[1:]), ((), ())), preferred_element_type=F32)


def running(ld):
    tok = ld.shape[1]
    row = lax.broadcasted_iota(jnp.int32, (tok, tok), 0)
    col = lax.broadcasted_iota(jnp.int32, (tok, tok), 1)
    upper = (row <= col).astype(F32).astype(BF16)
    high = ld.astype(BF16)
    rest = ld - high.astype(F32)
    mid = rest.astype(BF16)
    low = (rest - mid.astype(F32)).astype(BF16)
    return dot(high, upper) + (dot(mid, upper) + dot(low, upper))


def start_kernel(cap, experts, ld_ref, ids_ref, dep, cum_ref, target_ref):
    cum_ref[...] = running(ld_ref[...])
    top, tok = ids_ref.shape
    ids = ids_ref[...]
    expert = lax.broadcasted_iota(jnp.int32, (experts, tok), 0)
    hot = [(ids[k : k + 1, :] == expert).astype(F32) for k in range(top)]
    row = lax.broadcasted_iota(jnp.int32, (tok, tok), 0)
    col = lax.broadcasted_iota(jnp.int32, (tok, tok), 1)
    count = dot(sum(hot).astype(BF16), (row < col).astype(F32).astype(BF16))
    for k in range(top):
        slot = jnp.sum(hot[k] * count, axis=0, keepdims=True).astype(jnp.int32)
        target_ref[k : k + 1, :] = ids[k : k + 1, :] * cap + slot
        count = count + hot[k]


def start(log_decay, ids, dep, cap, experts):
    return pl.pallas_call(
        functools.partial(start_kernel, cap, experts),
        in_specs=[VMEM] * 2 + [ANY],
        out_specs=[VMEM] * 2,
        out_shape=[jax.ShapeDtypeStruct(a.shape, a.dtype) for a in (log_decay, ids)],
        compiler_params=pltpu.CompilerParams(vmem_limit_bytes=16 << 20),
        cost_estimate=BRIEF,
        name="start",
    )(log_decay, ids, dep)


def group_rows(cum, group, first, count):
    size = cum.shape[0] // SLOTS
    rows = cum[first : first + count]
    for g in range(1, SLOTS):
        rows = jnp.where(group == g, cum[g * size + first : g * size + first + count], rows)
    return rows


def state_kernel(first_slot, chunk, hd, place, k_ref, v_ref, ld_ref, dep, out):
    per = out.shape[1]
    cum = running(ld_ref[...])
    for j in range(2):
        group = jnp.bitwise_xor(j + first_slot, place[0])
        rows = group_rows(cum, group, chunk * per, per)
        total = rows[:, -1:]
        weight = jnp.exp(total - rows)
        decay = jnp.exp(total)
        for i in range(per):
            cols = pl.ds(pl.multiple_of(((group * CHUNKS + chunk) * per + i) * hd, hd), hd)
            wk = (weight[i : i + 1, :] * k_ref[:, cols].T.astype(F32)).astype(BF16)
            out[j, i, :hd, :] = dot(wk, v_ref[:, cols])
            out[j, i, hd:, :] = jnp.broadcast_to(decay[i : i + 1, :], (TAIL, hd))


def block_states(place, key_rows, value_rows, log_decay, dep, first_slot, chunk, hd):
    per = key_rows.shape[1] // SLOTS // CHUNKS // hd
    return pl.pallas_call(
        functools.partial(state_kernel, first_slot, chunk, hd),
        in_specs=[SMEM] + [VMEM] * 3 + [ANY],
        out_specs=VMEM,
        out_shape=jax.ShapeDtypeStruct((2, per, hd + TAIL, hd), F32),
        compiler_params=pltpu.CompilerParams(vmem_limit_bytes=16 << 20),
        cost_estimate=BRIEF,
        name="block_states",
    )(place, key_rows, value_rows, log_decay, dep)


def intra_kernel(hd, slot, place, q_ref, k_ref, v_ref, cum_ref, dep, *outs):
    tok, cw = outs[0].shape
    per = cw // hd
    gh = per * CHUNKS
    half = tok // 2
    group = jnp.bitwise_xor(slot, place[0])
    cum_rows = group_rows(cum_ref[...], group, 0, gh)
    cum = cum_rows.T
    row = lax.broadcasted_iota(jnp.int32, (half, half), 0)
    col = lax.broadcasted_iota(jnp.int32, (half, half), 1)
    causal = row >= col
    for i in range(gh):
        cols = pl.ds(pl.multiple_of(group * (gh * hd) + i * hd, hd), hd)
        o_ref, to = outs[i // per], slice(i % per * hd, (i % per + 1) * hd)
        down, across = cum[:, i : i + 1], cum_rows[i : i + 1, :]
        q, k, v = q_ref[:, cols], k_ref[:, cols], v_ref[:, cols]
        score = dot(q, k, (1, 1))
        diagonal = []
        for first in (0, half):
            at = slice(first, first + half)
            diagonal.append(jnp.where(causal, score[at, at] * jnp.exp(down[at] - across[:, at]), 0.0).astype(BF16))
        middle = across[:, half - 1 : half]
        below = score[half:, :half] * (jnp.exp(down[half:] - middle) * jnp.exp(middle - across[:, :half]))
        weights = jnp.concatenate(
            [
                jnp.concatenate([diagonal[0], jnp.zeros((half, half), BF16)], axis=1),
                jnp.concatenate([below.astype(BF16), diagonal[1]], axis=1),
            ],
            axis=0,
        )
        o_ref[:, to] = dot(weights, v)


def intra(place, query, key_rows, value_rows, cum, dep, slot, hd):
    tok, width = query.shape
    cw = width // SLOTS // CHUNKS
    return pl.pallas_call(
        functools.partial(intra_kernel, hd, slot),
        in_specs=[SMEM] + [VMEM] * 4 + [ANY],
        out_specs=[VMEM] * CHUNKS,
        out_shape=[jax.ShapeDtypeStruct((tok, cw), F32)] * CHUNKS,
        compiler_params=pltpu.CompilerParams(vmem_limit_bytes=16 << 20),
        cost_estimate=BRIEF,
        name="intra",
    )(place, query, key_rows, value_rows, cum, dep)


def add_branch(hd, chunk, slots, place, q_ref, gate_ref, ag_ref, cum_ref, states, ins, o_ref):
    per = states[0].shape[1]
    cw = per * hd
    squares = 0.0
    grown = jnp.exp(cum_ref[...])
    for n, slot in enumerate(slots):
        group = jnp.bitwise_xor(slot, place[0])
        grow = group_rows(grown, group, chunk * per, per).T
        for i in range(per):
            carried = states[n // 2][slot % 2, i]
            high = carried.astype(BF16)
            low = (carried - high.astype(F32)).astype(BF16)
            where = pl.ds(pl.multiple_of((group * CHUNKS + chunk) * cw + i * hd, hd), hd)
            q = q_ref[:, where]
            att = ins[n][:, i * hd : (i + 1) * hd] + grow[:, i : i + 1] * (dot(q, high) + dot(q, low))
            squares = squares + att * att
            opened = 0.5 * jnp.tanh(0.5 * gate_ref[:, where].astype(F32)) + 0.5
            o_ref[:, n * cw + i * hd : n * cw + (i + 1) * hd] = att * (ag_ref[:, where] * opened)
    return squares


def branch_kernel(hd, chunk, slots, place, q_ref, gate_ref, ag_ref, cum_ref, state, dep, *rest):
    o_ref, sq_ref = rest[-2:]
    sq_ref[...] = add_branch(
        hd, chunk, slots, place, q_ref, gate_ref, ag_ref, cum_ref, (state,), rest[:-2], o_ref
    )


def branch(place, query, gate, attn_gain, cum, states, intra_outs, dep, chunk, side, hd):
    tok, width = query.shape
    slots = (2 * side, 2 * side + 1)
    return pl.pallas_call(
        functools.partial(branch_kernel, hd, chunk, slots),
        in_specs=[SMEM] + [VMEM] * 5 + [ANY] + [VMEM] * 2,
        out_specs=[VMEM] * 2,
        out_shape=[
            jax.ShapeDtypeStruct((tok, 2 * (width // SLOTS // CHUNKS)), F32),
            jax.ShapeDtypeStruct((tok, hd), F32),
        ],
        compiler_params=pltpu.CompilerParams(vmem_limit_bytes=16 << 20),
        cost_estimate=BRIEF,
        name="branch",
    )(place, query, gate, attn_gain, cum, states[side], dep, *[intra_outs[j][chunk] for j in slots])


def finish_kernel(hd, place, q_ref, gate_ref, ag_ref, cum_ref, there, dep, *rest):
    ins, rest = rest[:2], rest[2:]
    count = 2 * CHUNKS - 1
    early, squares, rest = rest[:count], rest[count : 2 * count], rest[2 * count :]
    res_ref, mg_ref, target, o_ref, late, sq, sums, hidden, normed, pick = rest
    tok, width = normed.shape
    per = there.shape[1]
    cw = per * hd
    top = target.shape[0]

    part = add_branch(
        hd, CHUNKS - 1, (2, 3), place, q_ref, gate_ref, ag_ref, cum_ref, (there,), ins, late
    )
    for s in squares:
        part = part + s[...]
    rows = tok // 4
    scale = lax.rsqrt(jnp.sum(part, axis=-1, keepdims=True) / width + 1e-06)
    sq[...] = jnp.broadcast_to(scale, sq.shape)

    @pl.loop(0, tok // rows)
    def _(step):
        at = pl.ds(pl.multiple_of(step * rows, rows), rows)
        scale = sq[at, :]
        total = jnp.zeros((rows, LANES), F32)
        for slot in range(SLOTS):
            group = jnp.bitwise_xor(slot, place[0])
            for k in range(CHUNKS):
                for n in range(cw // LANES):
                    source = (*early, late)[2 * k + slot // 2]
                    here = slice(slot % 2 * cw + n * LANES, slot % 2 * cw + (n + 1) * LANES)
                    where = pl.ds(pl.multiple_of((group * CHUNKS + k) * cw + n * LANES, LANES), LANES)
                    value = source[at, here]
                    value = res_ref[at, where].astype(F32) + value * scale
                    total = total + value * value
                    hidden[at, where] = value
        sums[at, :] = total

    scale = lax.rsqrt(jnp.sum(sums[...], axis=-1, keepdims=True) / width + 1e-06)
    sq[...] = jnp.broadcast_to(scale, sq.shape)

    row = lax.broadcasted_iota(jnp.int32, (o_ref.shape[0], tok), 0)
    hit = row == target[0:1, :]
    for k in range(1, top):
        hit = hit | (row == target[k : k + 1, :])
    pick[...] = hit.astype(F32).astype(BF16)
    for n in range(0, width, 2 * LANES):
        cols = slice(n, n + 2 * LANES)
        for at in (slice(n, n + LANES), slice(n + LANES, n + 2 * LANES)):
            normed[:, at] = (hidden[:, at] * sq[...] * mg_ref[:, at]).astype(BF16)
        o_ref[:, cols] = dot(pick[...], normed[:, cols]).astype(BF16)


def finish(place, query, gate, attn_gain, cum, there, intra_outs, early, squares, residual, moe_gain, target, dep, rows, hd):
    tok, width = query.shape
    return pl.pallas_call(
        functools.partial(finish_kernel, hd),
        in_specs=[SMEM] + [VMEM] * 5 + [ANY] + [VMEM] * (2 + 2 * (2 * CHUNKS - 1) + 3),
        out_specs=VMEM,
        scratch_shapes=[
            pltpu.VMEM((tok, width // CHUNKS // 2), F32),
            pltpu.VMEM((tok, LANES), F32),
            pltpu.VMEM((tok, LANES), F32),
            pltpu.VMEM((tok, width), F32),
            pltpu.VMEM((tok, width), BF16),
            pltpu.VMEM((rows, tok), BF16),
        ],
        out_shape=jax.ShapeDtypeStruct((rows, width), BF16),
        compiler_params=pltpu.CompilerParams(vmem_limit_bytes=28 << 20),
        cost_estimate=BRIEF,
        name="finish",
    )(
        place, query, gate, attn_gain, cum, there, dep, *[o[-1] for o in intra_outs[2:]],
        *early, *squares, residual, moe_gain, target,
    )


def land_kernel(i_ref, o_ref, sems):
    steps = sems.shape[0]
    rows = i_ref.shape[0] // steps
    copies = [
        pltpu.make_async_copy(
            i_ref.at[pl.ds(n * rows, rows)], o_ref.at[0, pl.ds(n * rows, rows)], sems.at[n]
        )
        for n in range(steps)
    ]
    for c in copies:
        c.start()
    for c in copies:
        c.wait()


def land(arrived):
    return pl.pallas_call(
        land_kernel,
        in_specs=[ANY],
        out_specs=ANY,
        scratch_shapes=[pltpu.SemaphoreType.DMA((8,))],
        out_shape=jax.ShapeDtypeStruct((1,) + arrived.shape, arrived.dtype),
        compiler_params=pltpu.CompilerParams(vmem_limit_bytes=16 << 20),
        cost_estimate=BRIEF,
        name="land",
    )(arrived)


def swap(value, bit):
    size = lax.axis_size("ctx")
    return lax.ppermute(value, "ctx", [(i, i ^ bit) for i in range(size)])


def small(kernel, name, flags, ins, dep, outs):
    return pl.pallas_call(
        kernel,
        in_specs=[SMEM] + [VMEM] * len(ins) + [ANY],
        out_specs=[VMEM] * len(outs),
        out_shape=[jax.ShapeDtypeStruct(shape, kind) for shape, kind in outs],
        compiler_params=pltpu.CompilerParams(vmem_limit_bytes=16 << 20),
        cost_estimate=BRIEF,
        name=name,
    )(flags, *ins, dep)


def later(before, decay, state):
    return decay * before + state


def decay_rows(decay, rows):
    high = decay.astype(BF16).astype(F32)
    mid = (decay - high).astype(BF16).astype(F32)
    low = decay - high - mid
    row = lax.broadcasted_iota(jnp.int32, (decay.shape[0], rows, decay.shape[2]), 1)
    return jnp.where(row == 0, high, jnp.where(row == 1, mid, jnp.where(row == 2, low, 0.0)))


def chip_kernel(flags, keep, received, dep, mine, sent, rest):
    hd = keep.shape[-1]
    low = flags[1] == 0
    for slot in range(2):
        a = jnp.where(low, keep[slot], received[slot])
        b = jnp.where(low, received[slot], keep[slot])
        state = later(a[:, :hd, :], b[:, hd : hd + 1, :], b[:, :hd, :])
        decay = a[:, hd:, :] * b[:, hd:, :]
        if slot == 0:
            mine[:, :hd, :] = state
            mine[:, hd:, :] = decay
        else:
            high = state.astype(BF16)
            sent[:, :hd, :] = high
            sent[:, hd:, :] = decay_rows(decay[:, :1, :], 2 * TAIL).astype(BF16)
            rest[...] = (state - high.astype(F32)).astype(BF16)


def late_kernel(flags, *refs):
    count = len(refs) // 2
    for i_ref, o_ref in zip(refs[:count], refs[count + 1 :]):
        o_ref[...] = i_ref[...]


def row_parts(flags, mine, other, rest=None):
    hd = mine.shape[-1]
    low = flags[2] == 0
    a = (mine[:, :hd, :], mine[:, hd : hd + 1, :])
    state = other[:, :hd, :].astype(F32)
    if rest is not None:
        state = state + rest[...].astype(F32)
    b = (state, jnp.sum(other[:, hd:, :].astype(F32), axis=1, keepdims=True))
    first = tuple(jnp.where(low, x, y) for x, y in zip(a, b))
    second = tuple(jnp.where(low, y, x) for x, y in zip(a, b))
    return first, second


def row_kernel(flags, mine, other, dep, sent):
    first, second = row_parts(flags, mine, other)
    sent[...] = later(first[0], second[1], second[0]).astype(sent.dtype)


def arrived_sum(refs):
    return sum(r[...].astype(F32) for r in refs)


def hop_kernel(flags, mine, other, rest, *more):
    hops, sent = more[:-2], more[-1]
    first, second = row_parts(flags, mine, other, rest)
    total = later(first[0], second[1], second[0])
    sent[...] = later(arrived_sum(hops), first[1] * second[1], total).astype(sent.dtype)


def side_kernel(flags, mine, other, rest, *more):
    hops, (_, here, sent) = more[:-3], more[-3:]
    low = flags[2] == 0
    first, _ = row_parts(flags, mine, other, rest)
    before = arrived_sum(hops)
    entered = later(before, first[1], first[0])
    here[...] = jnp.where(low, before, entered)
    sent[...] = jnp.where(low, entered, before).astype(sent.dtype)


def core_kernel(flags, keep, received, here, there, dep, own, sent):
    hd = keep.shape[-1]
    low = flags[1] == 0
    for slot, ref in ((0, here), (1, there)):
        pair = ref[...].astype(F32)
        first = jnp.where(low, keep[slot], received[slot])
        second = later(pair, first[:, hd : hd + 1, :], first[:, :hd, :])
        own[slot] = jnp.where(low, pair, second)
        sent[slot] = jnp.where(low, second, pair)


def body(
    query, key_rows, value_rows, log_decay, gate_input, residual, attn_gain, moe_gain, expert_ids
):
    tok_rows, model_width = query.shape
    heads = log_decay.shape[1]
    hd = model_width // heads
    per = heads // SLOTS // CHUNKS
    size = lax.axis_size("ctx")
    hops = size // SLOTS - 1
    index = lax.axis_index("ctx").astype(jnp.int32)
    core, side = jnp.bitwise_and(index, 1), jnp.bitwise_and(lax.shift_right_logical(index, 1), 1)
    place = (2 * core + side)[None]
    flags = jnp.stack([2 * core + side, core, side])
    expert_count = EXP_DEV * size
    capacity = 5 * tok_rows * expert_ids.shape[1] // (4 * expert_count)
    ld = log_decay.T
    ag, mg = attn_gain[None], moe_gain[None]
    full, wire, plain = (per, hd + TAIL, hd), (per, hd + 2 * TAIL, hd), (per, hd, hd)

    received, keep, mine, other, rest = [], [], [], [], []
    dep = ld

    def chip(k, dep):
        m, t, r = small(
            chip_kernel, "chip", flags, [keep[k], received[k]], dep, [(full, F32), (wire, BF16), (plain, BF16)]
        )
        mine.append(m)
        other.append(swap(t, 2))
        rest.append(r)
        return m

    for k in range(CHUNKS):
        dep = block_states(place, key_rows, value_rows, ld, dep, 2, k, hd)
        received.append(swap(dep, 1))
        if k == 1:
            cum, target = start(ld, expert_ids.T, dep, capacity, expert_count)
            dep = cum
        if k:
            dep = chip(k - 1, dep)
        dep = block_states(place, key_rows, value_rows, ld, dep, 0, k, hd)
        keep.append(dep)
    dep = chip(CHUNKS - 1, dep)

    intra_outs = []
    arrived = [[] for _ in range(CHUNKS)]
    here, there, states = [None] * CHUNKS, [None] * CHUNKS, [None] * CHUNKS
    early, squares = [], []

    def more_intra(dep):
        if len(intra_outs) < SLOTS:
            intra_outs.append(intra(place, query, key_rows, value_rows, cum, dep, len(intra_outs), hd))
            dep = intra_outs[-1][0]
        return dep

    def hop(k, sent):
        s = len(arrived[k])
        pairs = [(s * SLOTS + j, (s + 1) * SLOTS + j) for j in range(SLOTS)]
        arrived[k].append(lax.ppermute(sent, "ctx", pairs))

    dep = more_intra(dep)
    rest = small(late_kernel, "late", flags, rest, dep, [(plain, BF16)] * CHUNKS)
    dep = rest[0]
    rest = [swap(r, 2) for r in rest]
    order = sorted(((k, stage) for k in range(CHUNKS) for stage in range(hops + 2)), key=lambda r: r[1] + 0.6 * r[0])
    for k, stage in order:
        if stage == 0:
            (dep,) = small(row_kernel, "row", flags, [mine[k], other[k]], dep, [(plain, BF16)])
            hop(k, dep)
        elif stage < hops:
            (dep,) = small(
                hop_kernel, "hop", flags, [mine[k], other[k], rest[k]] + arrived[k], dep, [(plain, BF16)]
            )
            hop(k, dep)
        elif stage == hops:
            here[k], dep = small(
                side_kernel,
                "side",
                flags,
                [mine[k], other[k], rest[k]] + arrived[k],
                dep,
                [(plain, F32), (plain, BF16)],
            )
            there[k] = swap(dep, 2)
        else:
            own, dep = small(
                core_kernel, "core", flags, [keep[k], received[k], here[k], there[k]], dep, [((2,) + plain, F32)] * 2
            )
            states[k] = (own, swap(dep, 1))
            for chunk, half in ((k - 1, 1), (k, 0)):
                if chunk >= 0:
                    dep, sq = branch(place, query, gate_input, ag, cum, states[chunk], intra_outs, dep, chunk, half, hd)
                    early.append(dep)
                    squares.append(sq)
        dep = more_intra(dep)
    outgoing = finish(
        place, query, gate_input, ag, cum, states[-1][1], intra_outs, early, squares,
        residual, mg, target, dep, expert_count * capacity, hd,
    )
    return land(lax.all_to_all(outgoing, "ctx", split_axis=0, concat_axis=0, tiled=True))


def solution(mesh):
    rows = P(("groups", "ctx"), None)
    in_specs = (rows, rows, rows, rows, rows, rows, P(), P(), rows)
    out_specs = P(("groups", "ctx"), None, None)
    return jax.shard_map(body, mesh=mesh, in_specs=in_specs, out_specs=out_specs, check_vma=False)
```

```python
import functools
import jax
import jax.numpy as jnp
from jax import lax
from jax.experimental import pallas as pl
from jax.experimental.pallas import tpu as pltpu
from jax.sharding import PartitionSpec as P

EXP_DEV = 1
SLOTS = 4
CHUNKS = 2
LANES = 128
TAIL = 8
F32 = jnp.float32
BF16 = jnp.bfloat16
ANY = pl.BlockSpec(memory_space=pl.ANY)
VMEM = pl.BlockSpec(memory_space=pltpu.VMEM)
SMEM = pl.BlockSpec(memory_space=pltpu.SMEM)
BRIEF = pl.CostEstimate(flops=1, bytes_accessed=1, transcendentals=0)


def dot(a, b, contract=(1, 0)):
    return lax.dot_general(a, b, ((contract[:1], contract[1:]), ((), ())), preferred_element_type=F32)


def running(ld):
    tok = ld.shape[1]
    row = lax.broadcasted_iota(jnp.int32, (tok, tok), 0)
    col = lax.broadcasted_iota(jnp.int32, (tok, tok), 1)
    upper = (row <= col).astype(F32).astype(BF16)
    high = ld.astype(BF16)
    rest = ld - high.astype(F32)
    mid = rest.astype(BF16)
    low = (rest - mid.astype(F32)).astype(BF16)
    return dot(high, upper) + (dot(mid, upper) + dot(low, upper))


def start_kernel(cap, experts, ld_ref, ids_ref, dep, cum_ref, target_ref):
    cum_ref[...] = running(ld_ref[...])
    top, tok = ids_ref.shape
    ids = ids_ref[...]
    expert = lax.broadcasted_iota(jnp.int32, (experts, tok), 0)
    hot = [(ids[k : k + 1, :] == expert).astype(F32) for k in range(top)]
    row = lax.broadcasted_iota(jnp.int32, (tok, tok), 0)
    col = lax.broadcasted_iota(jnp.int32, (tok, tok), 1)
    count = dot(sum(hot).astype(BF16), (row < col).astype(F32).astype(BF16))
    for k in range(top):
        slot = jnp.sum(hot[k] * count, axis=0, keepdims=True).astype(jnp.int32)
        target_ref[k : k + 1, :] = ids[k : k + 1, :] * cap + slot
        count = count + hot[k]


def start(log_decay, ids, dep, cap, experts):
    return pl.pallas_call(
        functools.partial(start_kernel, cap, experts),
        in_specs=[VMEM] * 2 + [ANY],
        out_specs=[VMEM] * 2,
        out_shape=[jax.ShapeDtypeStruct(a.shape, a.dtype) for a in (log_decay, ids)],
        compiler_params=pltpu.CompilerParams(vmem_limit_bytes=16 << 20),
        cost_estimate=BRIEF,
        name="start",
    )(log_decay, ids, dep)


def group_rows(cum, group, first, count):
    size = cum.shape[0] // SLOTS
    rows = cum[first : first + count]
    for g in range(1, SLOTS):
        rows = jnp.where(group == g, cum[g * size + first : g * size + first + count], rows)
    return rows


def state_kernel(first_slot, chunk, hd, place, k_ref, v_ref, ld_ref, dep, out):
    per = out.shape[1]
    cum = running(ld_ref[...])
    for j in range(2):
        group = jnp.bitwise_xor(j + first_slot, place[0])
        rows = group_rows(cum, group, chunk * per, per)
        total = rows[:, -1:]
        weight = jnp.exp(total - rows)
        decay = jnp.exp(total)
        for i in range(per):
            cols = pl.ds(pl.multiple_of(((group * CHUNKS + chunk) * per + i) * hd, hd), hd)
            wk = (weight[i : i + 1, :] * k_ref[:, cols].T.astype(F32)).astype(BF16)
            out[j, i, :hd, :] = dot(wk, v_ref[:, cols])
            out[j, i, hd:, :] = jnp.broadcast_to(decay[i : i + 1, :], (TAIL, hd))


def block_states(place, key_rows, value_rows, log_decay, dep, first_slot, chunk, hd):
    per = key_rows.shape[1] // SLOTS // CHUNKS // hd
    return pl.pallas_call(
        functools.partial(state_kernel, first_slot, chunk, hd),
        in_specs=[SMEM] + [VMEM] * 3 + [ANY],
        out_specs=VMEM,
        out_shape=jax.ShapeDtypeStruct((2, per, hd + TAIL, hd), F32),
        compiler_params=pltpu.CompilerParams(vmem_limit_bytes=16 << 20),
        cost_estimate=BRIEF,
        name="block_states",
    )(place, key_rows, value_rows, log_decay, dep)


def intra_kernel(hd, slot, place, q_ref, k_ref, v_ref, cum_ref, dep, *outs):
    tok, cw = outs[0].shape
    per = cw // hd
    gh = per * CHUNKS
    half = tok // 2
    group = jnp.bitwise_xor(slot, place[0])
    cum_rows = group_rows(cum_ref[...], group, 0, gh)
    cum = cum_rows.T
    row = lax.broadcasted_iota(jnp.int32, (half, half), 0)
    col = lax.broadcasted_iota(jnp.int32, (half, half), 1)
    causal = row >= col
    for i in range(gh):
        cols = pl.ds(pl.multiple_of(group * (gh * hd) + i * hd, hd), hd)
        o_ref, to = outs[i // per], slice(i % per * hd, (i % per + 1) * hd)
        down, across = cum[:, i : i + 1], cum_rows[i : i + 1, :]
        q, k, v = q_ref[:, cols], k_ref[:, cols], v_ref[:, cols]
        score = dot(q, k, (1, 1))
        diagonal = []
        for first in (0, half):
            at = slice(first, first + half)
            diagonal.append(jnp.where(causal, score[at, at] * jnp.exp(down[at] - across[:, at]), 0.0).astype(BF16))
        middle = across[:, half - 1 : half]
        below = score[half:, :half] * (jnp.exp(down[half:] - middle) * jnp.exp(middle - across[:, :half]))
        weights = jnp.concatenate(
            [
                jnp.concatenate([diagonal[0], jnp.zeros((half, half), BF16)], axis=1),
                jnp.concatenate([below.astype(BF16), diagonal[1]], axis=1),
            ],
            axis=0,
        )
        o_ref[:, to] = dot(weights, v)


def intra(place, query, key_rows, value_rows, cum, dep, slot, hd):
    tok, width = query.shape
    cw = width // SLOTS // CHUNKS
    return pl.pallas_call(
        functools.partial(intra_kernel, hd, slot),
        in_specs=[SMEM] + [VMEM] * 4 + [ANY],
        out_specs=[VMEM] * CHUNKS,
        out_shape=[jax.ShapeDtypeStruct((tok, cw), F32)] * CHUNKS,
        compiler_params=pltpu.CompilerParams(vmem_limit_bytes=16 << 20),
        cost_estimate=BRIEF,
        name="intra",
    )(place, query, key_rows, value_rows, cum, dep)


def add_branch(hd, chunk, slots, place, q_ref, gate_ref, ag_ref, cum_ref, states, ins, o_ref):
    per = states[0].shape[1]
    cw = per * hd
    squares = 0.0
    grown = jnp.exp(cum_ref[...])
    for n, slot in enumerate(slots):
        group = jnp.bitwise_xor(slot, place[0])
        grow = group_rows(grown, group, chunk * per, per).T
        for i in range(per):
            carried = states[n // 2][slot % 2, i]
            high = carried.astype(BF16)
            low = (carried - high.astype(F32)).astype(BF16)
            where = pl.ds(pl.multiple_of((group * CHUNKS + chunk) * cw + i * hd, hd), hd)
            q = q_ref[:, where]
            att = ins[n][:, i * hd : (i + 1) * hd] + grow[:, i : i + 1] * (dot(q, high) + dot(q, low))
            squares = squares + att * att
            opened = 0.5 * jnp.tanh(0.5 * gate_ref[:, where].astype(F32)) + 0.5
            o_ref[:, n * cw + i * hd : n * cw + (i + 1) * hd] = att * (ag_ref[:, where] * opened)
    return squares


def branch_kernel(hd, chunk, slots, place, q_ref, gate_ref, ag_ref, cum_ref, state, dep, *rest):
    o_ref, sq_ref = rest[-2:]
    sq_ref[...] = add_branch(
        hd, chunk, slots, place, q_ref, gate_ref, ag_ref, cum_ref, (state,), rest[:-2], o_ref
    )


def branch(place, query, gate, attn_gain, cum, states, intra_outs, dep, chunk, side, hd):
    tok, width = query.shape
    slots = (2 * side, 2 * side + 1)
    return pl.pallas_call(
        functools.partial(branch_kernel, hd, chunk, slots),
        in_specs=[SMEM] + [VMEM] * 5 + [ANY] + [VMEM] * 2,
        out_specs=[VMEM] * 2,
        out_shape=[
            jax.ShapeDtypeStruct((tok, 2 * (width // SLOTS // CHUNKS)), F32),
            jax.ShapeDtypeStruct((tok, hd), F32),
        ],
        compiler_params=pltpu.CompilerParams(vmem_limit_bytes=16 << 20),
        cost_estimate=BRIEF,
        name="branch",
    )(place, query, gate, attn_gain, cum, states[side], dep, *[intra_outs[j][chunk] for j in slots])


def finish_kernel(hd, place, q_ref, gate_ref, ag_ref, cum_ref, there, dep, *rest):
    ins, rest = rest[:2], rest[2:]
    count = 2 * CHUNKS - 1
    early, squares, rest = rest[:count], rest[count : 2 * count], rest[2 * count :]
    res_ref, mg_ref, target, o_ref, late, sq, sums, hidden, normed, pick = rest
    tok, width = normed.shape
    per = there.shape[1]
    cw = per * hd
    top = target.shape[0]

    part = add_branch(
        hd, CHUNKS - 1, (2, 3), place, q_ref, gate_ref, ag_ref, cum_ref, (there,), ins, late
    )
    for s in squares:
        part = part + s[...]
    rows = tok // 4
    scale = lax.rsqrt(jnp.sum(part, axis=-1, keepdims=True) / width + 1e-06)
    sq[...] = jnp.broadcast_to(scale, sq.shape)

    @pl.loop(0, tok // rows)
    def _(step):
        at = pl.ds(pl.multiple_of(step * rows, rows), rows)
        scale = sq[at, :]
        total = jnp.zeros((rows, LANES), F32)
        for slot in range(SLOTS):
            group = jnp.bitwise_xor(slot, place[0])
            for k in range(CHUNKS):
                for n in range(cw // LANES):
                    source = (*early, late)[2 * k + slot // 2]
                    here = slice(slot % 2 * cw + n * LANES, slot % 2 * cw + (n + 1) * LANES)
                    where = pl.ds(pl.multiple_of((group * CHUNKS + k) * cw + n * LANES, LANES), LANES)
                    value = source[at, here]
                    value = res_ref[at, where].astype(F32) + value * scale
                    total = total + value * value
                    hidden[at, where] = value
        sums[at, :] = total

    scale = lax.rsqrt(jnp.sum(sums[...], axis=-1, keepdims=True) / width + 1e-06)
    sq[...] = jnp.broadcast_to(scale, sq.shape)

    row = lax.broadcasted_iota(jnp.int32, (o_ref.shape[0], tok), 0)
    hit = row == target[0:1, :]
    for k in range(1, top):
        hit = hit | (row == target[k : k + 1, :])
    pick[...] = hit.astype(F32).astype(BF16)
    for n in range(0, width, 2 * LANES):
        cols = slice(n, n + 2 * LANES)
        for at in (slice(n, n + LANES), slice(n + LANES, n + 2 * LANES)):
            normed[:, at] = (hidden[:, at] * sq[...] * mg_ref[:, at]).astype(BF16)
        o_ref[:, cols] = dot(pick[...], normed[:, cols]).astype(BF16)


def finish(place, query, gate, attn_gain, cum, there, intra_outs, early, squares, residual, moe_gain, target, dep, rows, hd):
    tok, width = query.shape
    return pl.pallas_call(
        functools.partial(finish_kernel, hd),
        in_specs=[SMEM] + [VMEM] * 5 + [ANY] + [VMEM] * (2 + 2 * (2 * CHUNKS - 1) + 3),
        out_specs=VMEM,
        scratch_shapes=[
            pltpu.VMEM((tok, width // CHUNKS // 2), F32),
            pltpu.VMEM((tok, LANES), F32),
            pltpu.VMEM((tok, LANES), F32),
            pltpu.VMEM((tok, width), F32),
            pltpu.VMEM((tok, width), BF16),
            pltpu.VMEM((rows, tok), BF16),
        ],
        out_shape=jax.ShapeDtypeStruct((rows, width), BF16),
        compiler_params=pltpu.CompilerParams(vmem_limit_bytes=28 << 20),
        cost_estimate=BRIEF,
        name="finish",
    )(
        place, query, gate, attn_gain, cum, there, dep, *[o[-1] for o in intra_outs[2:]],
        *early, *squares, residual, moe_gain, target,
    )


def land_kernel(i_ref, o_ref, sems):
    steps = sems.shape[0]
    rows = i_ref.shape[0] // steps
    copies = [
        pltpu.make_async_copy(
            i_ref.at[pl.ds(n * rows, rows)], o_ref.at[0, pl.ds(n * rows, rows)], sems.at[n]
        )
        for n in range(steps)
    ]
    for c in copies:
        c.start()
    for c in copies:
        c.wait()


def land(arrived):
    return pl.pallas_call(
        land_kernel,
        in_specs=[ANY],
        out_specs=ANY,
        scratch_shapes=[pltpu.SemaphoreType.DMA((8,))],
        out_shape=jax.ShapeDtypeStruct((1,) + arrived.shape, arrived.dtype),
        compiler_params=pltpu.CompilerParams(vmem_limit_bytes=16 << 20),
        cost_estimate=BRIEF,
        name="land",
    )(arrived)


def swap(value, bit):
    size = lax.axis_size("ctx")
    return lax.ppermute(value, "ctx", [(i, i ^ bit) for i in range(size)])


def small(kernel, name, flags, ins, dep, outs):
    return pl.pallas_call(
        kernel,
        in_specs=[SMEM] + [VMEM] * len(ins) + [ANY],
        out_specs=[VMEM] * len(outs),
        out_shape=[jax.ShapeDtypeStruct(shape, kind) for shape, kind in outs],
        compiler_params=pltpu.CompilerParams(vmem_limit_bytes=16 << 20),
        cost_estimate=BRIEF,
        name=name,
    )(flags, *ins, dep)


def later(before, decay, state):
    return decay * before + state


def decay_rows(decays, rows):
    row = lax.broadcasted_iota(jnp.int32, (rows, decays[0].shape[1]), 0)
    out = jnp.zeros(row.shape, F32)
    for i, decay in enumerate(decays):
        high = decay.astype(BF16).astype(F32)
        mid = (decay - high).astype(BF16).astype(F32)
        for n, part in enumerate((high, mid, decay - high - mid)):
            out = jnp.where(row == 3 * i + n, part, out)
    return out


def chip_kernel(flags, keep, received, dep, mine, sent, rest):
    hd = keep.shape[-1]
    low = flags[1] == 0
    for slot in range(2):
        a = jnp.where(low, keep[slot], received[slot])
        b = jnp.where(low, received[slot], keep[slot])
        state = later(a[:, :hd, :], b[:, hd : hd + 1, :], b[:, :hd, :])
        decay = a[:, hd:, :] * b[:, hd:, :]
        if slot == 0:
            mine[:, :hd, :] = state
            mine[:, hd:, :] = decay
        else:
            high = state.astype(BF16)
            per = high.shape[0]
            for i in range(per):
                sent[i * hd : (i + 1) * hd, :] = high[i]
            decays = [decay[i, :1, :] for i in range(per)]
            sent[per * hd :, :] = decay_rows(decays, sent.shape[0] - per * hd).astype(BF16)
            rest[...] = (state - high.astype(F32)).astype(BF16)


def row_parts(flags, mine, other, rest=None):
    hd = mine.shape[-1]
    low = flags[2] == 0
    a = (mine[:, :hd, :], mine[:, hd : hd + 1, :])
    per = mine.shape[0]
    state = other[: per * hd, :].astype(F32).reshape(per, hd, hd)
    if rest is not None:
        state = state + rest[...].astype(F32)
    tail = other[per * hd :, :].astype(F32)
    decays = [tail[i : i + 1] + tail[i + 1 : i + 2] + tail[i + 2 : i + 3] for i in range(0, 3 * per, 3)]
    b = (state, jnp.stack(decays))
    first = tuple(jnp.where(low, x, y) for x, y in zip(a, b))
    second = tuple(jnp.where(low, y, x) for x, y in zip(a, b))
    return first, second


def row_kernel(flags, mine, other, dep, sent):
    first, second = row_parts(flags, mine, other)
    sent[...] = later(first[0], second[1], second[0]).astype(sent.dtype)


def arrived_sum(refs):
    return sum(r[...].astype(F32) for r in refs)


def hop_kernel(flags, mine, other, rest, *more):
    hops, sent = more[:-2], more[-1]
    first, second = row_parts(flags, mine, other, rest)
    total = later(first[0], second[1], second[0])
    sent[...] = later(arrived_sum(hops), first[1] * second[1], total).astype(sent.dtype)


def side_kernel(flags, mine, other, rest, *more):
    hops, (_, here, sent) = more[:-3], more[-3:]
    low = flags[2] == 0
    first, _ = row_parts(flags, mine, other, rest)
    before = arrived_sum(hops)
    entered = later(before, first[1], first[0])
    here[...] = jnp.where(low, before, entered)
    sent[...] = jnp.where(low, entered, before).astype(sent.dtype)


def core_kernel(flags, keep, received, here, there, dep, own, sent):
    hd = keep.shape[-1]
    low = flags[1] == 0
    for slot, ref in ((0, here), (1, there)):
        pair = ref[...].astype(F32)
        first = jnp.where(low, keep[slot], received[slot])
        second = later(pair, first[:, hd : hd + 1, :], first[:, :hd, :])
        own[slot] = jnp.where(low, pair, second)
        sent[slot] = jnp.where(low, second, pair)


def body(
    query, key_rows, value_rows, log_decay, gate_input, residual, attn_gain, moe_gain, expert_ids
):
    tok_rows, model_width = query.shape
    heads = log_decay.shape[1]
    hd = model_width // heads
    per = heads // SLOTS // CHUNKS
    size = lax.axis_size("ctx")
    hops = size // SLOTS - 1
    index = lax.axis_index("ctx").astype(jnp.int32)
    core, side = jnp.bitwise_and(index, 1), jnp.bitwise_and(lax.shift_right_logical(index, 1), 1)
    place = (2 * core + side)[None]
    flags = jnp.stack([2 * core + side, core, side])
    expert_count = EXP_DEV * size
    capacity = 5 * tok_rows * expert_ids.shape[1] // (4 * expert_count)
    ld = log_decay.T
    ag, mg = attn_gain[None], moe_gain[None]
    full, wire, plain = (per, hd + TAIL, hd), (per * hd + (3 * per + 15) // 16 * 16, hd), (per, hd, hd)

    received, keep, mine, other, rest = [], [], [], [], []
    dep = ld

    def chip(k, dep):
        m, t, r = small(
            chip_kernel, "chip", flags, [keep[k], received[k]], dep, [(full, F32), (wire, BF16), (plain, BF16)]
        )
        mine.append(m)
        other.append(swap(t, 2))
        rest.append(r)
        return m

    for k in range(CHUNKS):
        dep = block_states(place, key_rows, value_rows, ld, dep, 2, k, hd)
        received.append(swap(dep, 1))
        if k == 1:
            cum, target = start(ld, expert_ids.T, dep, capacity, expert_count)
            dep = cum
        if k:
            dep = chip(k - 1, dep)
        dep = block_states(place, key_rows, value_rows, ld, dep, 0, k, hd)
        keep.append(dep)
    dep = chip(CHUNKS - 1, dep)

    intra_outs = []
    arrived = [[] for _ in range(CHUNKS)]
    here, there, states = [None] * CHUNKS, [None] * CHUNKS, [None] * CHUNKS
    early, squares = [], []

    def more_intra(dep):
        if len(intra_outs) < SLOTS:
            intra_outs.append(intra(place, query, key_rows, value_rows, cum, dep, len(intra_outs), hd))
            dep = intra_outs[-1][0]
        return dep

    def hop(k, sent):
        s = len(arrived[k])
        pairs = [(s * SLOTS + j, (s + 1) * SLOTS + j) for j in range(SLOTS)]
        arrived[k].append(lax.ppermute(sent, "ctx", pairs))

    dep = more_intra(dep)
    rest = [swap(r, 2) for r in rest]
    order = sorted(((k, stage) for k in range(CHUNKS) for stage in range(hops + 2)), key=lambda r: r[1] + 0.6 * r[0])
    for k, stage in order:
        if stage == 0:
            (dep,) = small(row_kernel, "row", flags, [mine[k], other[k]], dep, [(plain, BF16)])
            hop(k, dep)
        elif stage < hops:
            (dep,) = small(
                hop_kernel, "hop", flags, [mine[k], other[k], rest[k]] + arrived[k], dep, [(plain, BF16)]
            )
            hop(k, dep)
        elif stage == hops:
            here[k], dep = small(
                side_kernel,
                "side",
                flags,
                [mine[k], other[k], rest[k]] + arrived[k],
                dep,
                [(plain, F32), (plain, BF16)],
            )
            there[k] = swap(dep, 2)
        else:
            own, dep = small(
                core_kernel, "core", flags, [keep[k], received[k], here[k], there[k]], dep, [((2,) + plain, F32)] * 2
            )
            states[k] = (own, swap(dep, 1))
            for chunk, half in ((k - 1, 1), (k, 0)):
                if chunk >= 0:
                    dep, sq = branch(place, query, gate_input, ag, cum, states[chunk], intra_outs, dep, chunk, half, hd)
                    early.append(dep)
                    squares.append(sq)
        dep = more_intra(dep)
    outgoing = finish(
        place, query, gate_input, ag, cum, states[-1][1], intra_outs, early, squares,
        residual, mg, target, dep, expert_count * capacity, hd,
    )
    return land(lax.all_to_all(outgoing, "ctx", split_axis=0, concat_axis=0, tiled=True))


def solution(mesh):
    rows = P(("groups", "ctx"), None)
    in_specs = (rows, rows, rows, rows, rows, rows, P(), P(), rows)
    out_specs = P(("groups", "ctx"), None, None)
    return jax.shard_map(body, mesh=mesh, in_specs=in_specs, out_specs=out_specs, check_vma=False)
```

```python
import functools
import jax
import jax.numpy as jnp
from jax import lax
from jax.experimental import pallas as pl
from jax.experimental.pallas import tpu as pltpu
from jax.sharding import PartitionSpec as P

EXP_DEV = 1
SLOTS = 4
CHUNKS = 2
LANES = 128
TAIL = 8
F32 = jnp.float32
BF16 = jnp.bfloat16
ANY = pl.BlockSpec(memory_space=pl.ANY)
VMEM = pl.BlockSpec(memory_space=pltpu.VMEM)
SMEM = pl.BlockSpec(memory_space=pltpu.SMEM)
BRIEF = pl.CostEstimate(flops=1, bytes_accessed=1, transcendentals=0)


def dot(a, b, contract=(1, 0)):
    return lax.dot_general(a, b, ((contract[:1], contract[1:]), ((), ())), preferred_element_type=F32)


def running(ld):
    tok = ld.shape[1]
    row = lax.broadcasted_iota(jnp.int32, (tok, tok), 0)
    col = lax.broadcasted_iota(jnp.int32, (tok, tok), 1)
    upper = (row <= col).astype(F32).astype(BF16)
    high = ld.astype(BF16)
    rest = ld - high.astype(F32)
    mid = rest.astype(BF16)
    low = (rest - mid.astype(F32)).astype(BF16)
    return dot(high, upper) + (dot(mid, upper) + dot(low, upper))


def start_kernel(cap, experts, ld_ref, ids_ref, dep, cum_ref, target_ref):
    cum_ref[...] = running(ld_ref[...])
    top, tok = ids_ref.shape
    ids = ids_ref[...]
    expert = lax.broadcasted_iota(jnp.int32, (experts, tok), 0)
    hot = [(ids[k : k + 1, :] == expert).astype(F32) for k in range(top)]
    row = lax.broadcasted_iota(jnp.int32, (tok, tok), 0)
    col = lax.broadcasted_iota(jnp.int32, (tok, tok), 1)
    count = dot(sum(hot).astype(BF16), (row < col).astype(F32).astype(BF16))
    for k in range(top):
        slot = jnp.sum(hot[k] * count, axis=0, keepdims=True).astype(jnp.int32)
        target_ref[k : k + 1, :] = ids[k : k + 1, :] * cap + slot
        count = count + hot[k]


def start(log_decay, ids, dep, cap, experts):
    return pl.pallas_call(
        functools.partial(start_kernel, cap, experts),
        in_specs=[VMEM] * 2 + [ANY],
        out_specs=[VMEM] * 2,
        out_shape=[jax.ShapeDtypeStruct(a.shape, a.dtype) for a in (log_decay, ids)],
        compiler_params=pltpu.CompilerParams(vmem_limit_bytes=16 << 20),
        cost_estimate=BRIEF,
        name="start",
    )(log_decay, ids, dep)


def group_rows(cum, group, first, count):
    size = cum.shape[0] // SLOTS
    rows = cum[first : first + count]
    for g in range(1, SLOTS):
        rows = jnp.where(group == g, cum[g * size + first : g * size + first + count], rows)
    return rows


def state_kernel(first_slot, chunk, hd, place, k_ref, v_ref, ld_ref, dep, out):
    per = out.shape[1]
    cum = running(ld_ref[...])
    for j in range(2):
        group = jnp.bitwise_xor(j + first_slot, place[0])
        rows = group_rows(cum, group, chunk * per, per)
        total = rows[:, -1:]
        weight = jnp.exp(total - rows)
        decay = jnp.exp(total)
        for i in range(per):
            cols = pl.ds(pl.multiple_of(((group * CHUNKS + chunk) * per + i) * hd, hd), hd)
            wk = (weight[i : i + 1, :] * k_ref[:, cols].T.astype(F32)).astype(BF16)
            out[j, i, :hd, :] = dot(wk, v_ref[:, cols])
            out[j, i, hd:, :] = jnp.broadcast_to(decay[i : i + 1, :], (TAIL, hd))


def block_states(place, key_rows, value_rows, log_decay, dep, first_slot, chunk, hd):
    per = key_rows.shape[1] // SLOTS // CHUNKS // hd
    return pl.pallas_call(
        functools.partial(state_kernel, first_slot, chunk, hd),
        in_specs=[SMEM] + [VMEM] * 3 + [ANY],
        out_specs=VMEM,
        out_shape=jax.ShapeDtypeStruct((2, per, hd + TAIL, hd), F32),
        compiler_params=pltpu.CompilerParams(vmem_limit_bytes=16 << 20),
        cost_estimate=BRIEF,
        name="block_states",
    )(place, key_rows, value_rows, log_decay, dep)


def intra_kernel(hd, slot, place, q_ref, k_ref, v_ref, cum_ref, dep, *outs):
    tok, cw = outs[0].shape
    per = cw // hd
    gh = per * CHUNKS
    half = tok // 2
    group = jnp.bitwise_xor(slot, place[0])
    cum_rows = group_rows(cum_ref[...], group, 0, gh)
    cum = cum_rows.T
    row = lax.broadcasted_iota(jnp.int32, (half, half), 0)
    col = lax.broadcasted_iota(jnp.int32, (half, half), 1)
    causal = row >= col
    for i in range(gh):
        cols = pl.ds(pl.multiple_of(group * (gh * hd) + i * hd, hd), hd)
        o_ref, to = outs[i // per], slice(i % per * hd, (i % per + 1) * hd)
        down, across = cum[:, i : i + 1], cum_rows[i : i + 1, :]
        q, k, v = q_ref[:, cols], k_ref[:, cols], v_ref[:, cols]
        score = dot(q, k, (1, 1))
        diagonal = []
        for first in (0, half):
            at = slice(first, first + half)
            diagonal.append(jnp.where(causal, score[at, at] * jnp.exp(down[at] - across[:, at]), 0.0).astype(BF16))
        middle = across[:, half - 1 : half]
        below = score[half:, :half] * (jnp.exp(down[half:] - middle) * jnp.exp(middle - across[:, :half]))
        weights = jnp.concatenate(
            [
                jnp.concatenate([diagonal[0], jnp.zeros((half, half), BF16)], axis=1),
                jnp.concatenate([below.astype(BF16), diagonal[1]], axis=1),
            ],
            axis=0,
        )
        o_ref[:, to] = dot(weights, v)


def intra(place, query, key_rows, value_rows, cum, dep, slot, hd):
    tok, width = query.shape
    cw = width // SLOTS // CHUNKS
    return pl.pallas_call(
        functools.partial(intra_kernel, hd, slot),
        in_specs=[SMEM] + [VMEM] * 4 + [ANY],
        out_specs=[VMEM] * CHUNKS,
        out_shape=[jax.ShapeDtypeStruct((tok, cw), F32)] * CHUNKS,
        compiler_params=pltpu.CompilerParams(vmem_limit_bytes=16 << 20),
        cost_estimate=BRIEF,
        name="intra",
    )(place, query, key_rows, value_rows, cum, dep)


def add_branch(hd, chunk, slots, place, q_ref, gate_ref, ag_ref, cum_ref, states, ins, o_ref):
    per = states[0].shape[1]
    cw = per * hd
    squares = 0.0
    grown = jnp.exp(cum_ref[...])
    for n, slot in enumerate(slots):
        group = jnp.bitwise_xor(slot, place[0])
        grow = group_rows(grown, group, chunk * per, per).T
        for i in range(per):
            carried = states[n // 2][slot % 2, i]
            high = carried.astype(BF16)
            low = (carried - high.astype(F32)).astype(BF16)
            where = pl.ds(pl.multiple_of((group * CHUNKS + chunk) * cw + i * hd, hd), hd)
            q = q_ref[:, where]
            att = ins[n][:, i * hd : (i + 1) * hd] + grow[:, i : i + 1] * (dot(q, high) + dot(q, low))
            squares = squares + att * att
            opened = 0.5 * jnp.tanh(0.5 * gate_ref[:, where].astype(F32)) + 0.5
            o_ref[:, n * cw + i * hd : n * cw + (i + 1) * hd] = att * (ag_ref[:, where] * opened)
    return squares


def branch_kernel(hd, chunk, slots, place, q_ref, gate_ref, ag_ref, cum_ref, state, dep, *rest):
    o_ref, sq_ref = rest[-2:]
    sq_ref[...] = add_branch(
        hd, chunk, slots, place, q_ref, gate_ref, ag_ref, cum_ref, (state,), rest[:-2], o_ref
    )


def branch(place, query, gate, attn_gain, cum, states, intra_outs, dep, chunk, side, hd):
    tok, width = query.shape
    slots = (2 * side, 2 * side + 1)
    return pl.pallas_call(
        functools.partial(branch_kernel, hd, chunk, slots),
        in_specs=[SMEM] + [VMEM] * 5 + [ANY] + [VMEM] * 2,
        out_specs=[VMEM] * 2,
        out_shape=[
            jax.ShapeDtypeStruct((tok, 2 * (width // SLOTS // CHUNKS)), F32),
            jax.ShapeDtypeStruct((tok, hd), F32),
        ],
        compiler_params=pltpu.CompilerParams(vmem_limit_bytes=16 << 20),
        cost_estimate=BRIEF,
        name="branch",
    )(place, query, gate, attn_gain, cum, states[side], dep, *[intra_outs[j][chunk] for j in slots])


def finish_kernel(hd, place, q_ref, gate_ref, ag_ref, cum_ref, there, dep, *rest):
    ins, rest = rest[:2], rest[2:]
    count = 2 * CHUNKS - 1
    early, squares, rest = rest[:count], rest[count : 2 * count], rest[2 * count :]
    res_ref, mg_ref, target, o_ref, late, sq, sums, hidden, normed, pick = rest
    tok, width = normed.shape
    per = there.shape[1]
    cw = per * hd
    top = target.shape[0]

    part = add_branch(
        hd, CHUNKS - 1, (2, 3), place, q_ref, gate_ref, ag_ref, cum_ref, (there,), ins, late
    )
    for s in squares:
        part = part + s[...]
    rows = tok // 4
    scale = lax.rsqrt(jnp.sum(part, axis=-1, keepdims=True) / width + 1e-06)
    sq[...] = jnp.broadcast_to(scale, sq.shape)

    @pl.loop(0, tok // rows)
    def _(step):
        at = pl.ds(pl.multiple_of(step * rows, rows), rows)
        scale = sq[at, :]
        total = jnp.zeros((rows, LANES), F32)
        for slot in range(SLOTS):
            group = jnp.bitwise_xor(slot, place[0])
            for k in range(CHUNKS):
                for n in range(cw // LANES):
                    source = (*early, late)[2 * k + slot // 2]
                    here = slice(slot % 2 * cw + n * LANES, slot % 2 * cw + (n + 1) * LANES)
                    where = pl.ds(pl.multiple_of((group * CHUNKS + k) * cw + n * LANES, LANES), LANES)
                    value = source[at, here]
                    value = res_ref[at, where].astype(F32) + value * scale
                    total = total + value * value
                    hidden[at, where] = value
        sums[at, :] = total

    scale = lax.rsqrt(jnp.sum(sums[...], axis=-1, keepdims=True) / width + 1e-06)
    sq[...] = jnp.broadcast_to(scale, sq.shape)

    row = lax.broadcasted_iota(jnp.int32, (o_ref.shape[0], tok), 0)
    hit = row == target[0:1, :]
    for k in range(1, top):
        hit = hit | (row == target[k : k + 1, :])
    pick[...] = hit.astype(F32).astype(BF16)
    for n in range(0, width, 2 * LANES):
        cols = slice(n, n + 2 * LANES)
        for at in (slice(n, n + LANES), slice(n + LANES, n + 2 * LANES)):
            normed[:, at] = (hidden[:, at] * sq[...] * mg_ref[:, at]).astype(BF16)
        o_ref[:, cols] = dot(pick[...], normed[:, cols]).astype(BF16)


def finish(place, query, gate, attn_gain, cum, there, intra_outs, early, squares, residual, moe_gain, target, dep, rows, hd):
    tok, width = query.shape
    return pl.pallas_call(
        functools.partial(finish_kernel, hd),
        in_specs=[SMEM] + [VMEM] * 5 + [ANY] + [VMEM] * (2 + 2 * (2 * CHUNKS - 1) + 3),
        out_specs=VMEM,
        scratch_shapes=[
            pltpu.VMEM((tok, width // CHUNKS // 2), F32),
            pltpu.VMEM((tok, LANES), F32),
            pltpu.VMEM((tok, LANES), F32),
            pltpu.VMEM((tok, width), F32),
            pltpu.VMEM((tok, width), BF16),
            pltpu.VMEM((rows, tok), BF16),
        ],
        out_shape=jax.ShapeDtypeStruct((rows, width), BF16),
        compiler_params=pltpu.CompilerParams(vmem_limit_bytes=28 << 20),
        cost_estimate=BRIEF,
        name="finish",
    )(
        place, query, gate, attn_gain, cum, there, dep, *[o[-1] for o in intra_outs[2:]],
        *early, *squares, residual, moe_gain, target,
    )


def land_kernel(i_ref, o_ref, sems):
    steps = sems.shape[0]
    rows = i_ref.shape[0] // steps
    copies = [
        pltpu.make_async_copy(
            i_ref.at[pl.ds(n * rows, rows)], o_ref.at[0, pl.ds(n * rows, rows)], sems.at[n]
        )
        for n in range(steps)
    ]
    for c in copies:
        c.start()
    for c in copies:
        c.wait()


def land(arrived):
    return pl.pallas_call(
        land_kernel,
        in_specs=[ANY],
        out_specs=ANY,
        scratch_shapes=[pltpu.SemaphoreType.DMA((8,))],
        out_shape=jax.ShapeDtypeStruct((1,) + arrived.shape, arrived.dtype),
        compiler_params=pltpu.CompilerParams(vmem_limit_bytes=16 << 20),
        cost_estimate=BRIEF,
        name="land",
    )(arrived)


def swap(value, bit):
    size = lax.axis_size("ctx")
    return lax.ppermute(value, "ctx", [(i, i ^ bit) for i in range(size)])


def small(kernel, name, flags, ins, dep, outs):
    return pl.pallas_call(
        kernel,
        in_specs=[SMEM] + [VMEM] * len(ins) + [ANY],
        out_specs=[VMEM] * len(outs),
        out_shape=[jax.ShapeDtypeStruct(shape, kind) for shape, kind in outs],
        compiler_params=pltpu.CompilerParams(vmem_limit_bytes=16 << 20),
        cost_estimate=BRIEF,
        name=name,
    )(flags, *ins, dep)


def later(before, decay, state):
    return decay * before + state


def decay_rows(decays, rows):
    row = lax.broadcasted_iota(jnp.int32, (rows, decays[0].shape[1]), 0)
    out = jnp.zeros(row.shape, F32)
    for i, decay in enumerate(decays):
        high = decay.astype(BF16).astype(F32)
        mid = (decay - high).astype(BF16).astype(F32)
        for n, part in enumerate((high, mid, decay - high - mid)):
            out = jnp.where(row == 3 * i + n, part, out)
    return out


def chip_kernel(flags, keep, received, dep, mine, sent, rest):
    hd = keep.shape[-1]
    low = flags[1] == 0
    for slot in range(2):
        a = jnp.where(low, keep[slot], received[slot])
        b = jnp.where(low, received[slot], keep[slot])
        state = later(a[:, :hd, :], b[:, hd : hd + 1, :], b[:, :hd, :])
        decay = a[:, hd:, :] * b[:, hd:, :]
        if slot == 0:
            mine[:, :hd, :] = state
            mine[:, hd:, :] = decay
        else:
            high = state.astype(BF16)
            per = high.shape[0]
            for i in range(per):
                sent[i * hd : (i + 1) * hd, :] = high[i]
            decays = [decay[i, :1, :] for i in range(per)]
            sent[per * hd :, :] = decay_rows(decays, sent.shape[0] - per * hd).astype(BF16)
            rest[...] = (state - high.astype(F32)).astype(BF16)


def row_parts(flags, mine, other, rest=None):
    hd = mine.shape[-1]
    low = flags[2] == 0
    a = (mine[:, :hd, :], mine[:, hd : hd + 1, :])
    per = mine.shape[0]
    state = other[: per * hd, :].astype(F32).reshape(per, hd, hd)
    if rest is not None:
        state = state + rest[...].astype(F32)
    tail = other[per * hd :, :].astype(F32)
    decays = [tail[i : i + 1] + tail[i + 1 : i + 2] + tail[i + 2 : i + 3] for i in range(0, 3 * per, 3)]
    b = (state, jnp.stack(decays))
    first = tuple(jnp.where(low, x, y) for x, y in zip(a, b))
    second = tuple(jnp.where(low, y, x) for x, y in zip(a, b))
    return first, second


def row_kernel(flags, mine, other, dep, sent):
    first, second = row_parts(flags, mine, other)
    sent[...] = later(first[0], second[1], second[0]).astype(sent.dtype)


def arrived_sum(refs):
    return sum(r[...].astype(F32) for r in refs)


def hop_kernel(flags, mine, other, rest, *more):
    hops, sent = more[:-2], more[-1]
    first, second = row_parts(flags, mine, other, rest)
    total = later(first[0], second[1], second[0])
    sent[...] = later(arrived_sum(hops), first[1] * second[1], total).astype(sent.dtype)


def side_kernel(flags, mine, other, rest, *more):
    hops, (_, here, sent) = more[:-3], more[-3:]
    low = flags[2] == 0
    first, _ = row_parts(flags, mine, other, rest)
    before = arrived_sum(hops)
    entered = later(before, first[1], first[0])
    here[...] = jnp.where(low, before, entered)
    sent[...] = jnp.where(low, entered, before).astype(sent.dtype)


def core_kernel(flags, keep, received, here, there, dep, own, sent):
    hd = keep.shape[-1]
    low = flags[1] == 0
    for slot, ref in ((0, here), (1, there)):
        pair = ref[...].astype(F32)
        first = jnp.where(low, keep[slot], received[slot])
        second = later(pair, first[:, hd : hd + 1, :], first[:, :hd, :])
        own[slot] = jnp.where(low, pair, second)
        sent[slot] = jnp.where(low, second, pair)


def body(
    query, key_rows, value_rows, log_decay, gate_input, residual, attn_gain, moe_gain, expert_ids
):
    tok_rows, model_width = query.shape
    heads = log_decay.shape[1]
    hd = model_width // heads
    per = heads // SLOTS // CHUNKS
    size = lax.axis_size("ctx")
    hops = size // SLOTS - 1
    index = lax.axis_index("ctx").astype(jnp.int32)
    core, side = jnp.bitwise_and(index, 1), jnp.bitwise_and(lax.shift_right_logical(index, 1), 1)
    place = (2 * core + side)[None]
    flags = jnp.stack([2 * core + side, core, side])
    expert_count = EXP_DEV * size
    capacity = 5 * tok_rows * expert_ids.shape[1] // (4 * expert_count)
    ld = log_decay.T
    ag, mg = attn_gain[None], moe_gain[None]
    full, wire, plain = (per, hd + TAIL, hd), (per * hd + (3 * per + 15) // 16 * 16, hd), (per, hd, hd)

    received, keep, mine, other, rest = [], [], [], [], []
    dep = ld

    def chip(k, dep):
        m, t, r = small(
            chip_kernel, "chip", flags, [keep[k], received[k]], dep, [(full, F32), (wire, BF16), (plain, BF16)]
        )
        mine.append(m)
        other.append(swap(t, 2))
        rest.append(r)
        return m

    for k in range(CHUNKS):
        dep = block_states(place, key_rows, value_rows, ld, dep, 2, k, hd)
        received.append(swap(dep, 1))
    cum, target = start(ld, expert_ids.T, dep, capacity, expert_count)
    dep = cum
    for k in range(CHUNKS):
        if k:
            dep = chip(k - 1, dep)
        dep = block_states(place, key_rows, value_rows, ld, dep, 0, k, hd)
        keep.append(dep)
    dep = chip(CHUNKS - 1, dep)

    intra_outs = []
    arrived = [[] for _ in range(CHUNKS)]
    here, there, states = [None] * CHUNKS, [None] * CHUNKS, [None] * CHUNKS
    early, squares = [], []

    def more_intra(dep):
        if len(intra_outs) < SLOTS:
            intra_outs.append(intra(place, query, key_rows, value_rows, cum, dep, len(intra_outs), hd))
            dep = intra_outs[-1][0]
        return dep

    def hop(k, sent):
        s = len(arrived[k])
        pairs = [(s * SLOTS + j, (s + 1) * SLOTS + j) for j in range(SLOTS)]
        arrived[k].append(lax.ppermute(sent, "ctx", pairs))

    dep = more_intra(dep)
    rest = [swap(r, 2) for r in rest]
    order = sorted(((k, stage) for k in range(CHUNKS) for stage in range(hops + 2)), key=lambda r: r[1] + 0.6 * r[0])
    for k, stage in order:
        if stage == 0:
            (dep,) = small(row_kernel, "row", flags, [mine[k], other[k]], dep, [(plain, BF16)])
            hop(k, dep)
        elif stage < hops:
            (dep,) = small(
                hop_kernel, "hop", flags, [mine[k], other[k], rest[k]] + arrived[k], dep, [(plain, BF16)]
            )
            hop(k, dep)
        elif stage == hops:
            here[k], dep = small(
                side_kernel,
                "side",
                flags,
                [mine[k], other[k], rest[k]] + arrived[k],
                dep,
                [(plain, F32), (plain, BF16)],
            )
            there[k] = swap(dep, 2)
        else:
            own, dep = small(
                core_kernel, "core", flags, [keep[k], received[k], here[k], there[k]], dep, [((2,) + plain, F32)] * 2
            )
            states[k] = (own, swap(dep, 1))
            for chunk, half in ((k - 1, 1), (k, 0)):
                if chunk >= 0:
                    dep, sq = branch(place, query, gate_input, ag, cum, states[chunk], intra_outs, dep, chunk, half, hd)
                    early.append(dep)
                    squares.append(sq)
        dep = more_intra(dep)
    outgoing = finish(
        place, query, gate_input, ag, cum, states[-1][1], intra_outs, early, squares,
        residual, mg, target, dep, expert_count * capacity, hd,
    )
    return land(lax.all_to_all(outgoing, "ctx", split_axis=0, concat_axis=0, tiled=True))


def solution(mesh):
    rows = P(("groups", "ctx"), None)
    in_specs = (rows, rows, rows, rows, rows, rows, P(), P(), rows)
    out_specs = P(("groups", "ctx"), None, None)
    return jax.shard_map(body, mesh=mesh, in_specs=in_specs, out_specs=out_specs, check_vma=False)
```
